32 devices in a mesh: sp: 8 (over z, x), hd: 4 (over y, core).
Axes of the slice: x: 2, y: 2, z: 4, core: 2. Of those that a mesh axis runs over, the one named last changes fastest.
Arguments:
- cond: bfloat16 [8, 64, 64, 192], P('hd', 'sp'), may hold values from -6 to 6
- resid: bfloat16 [8, 64, 64, 320], P('hd', 'sp'), may hold values from -6 to 6
- context: bfloat16 [8, 1, 77, 768], P('hd'), may hold values from -6 to 6
- noise: float32 [8, 64, 64, 4], P('hd', 'sp'), may hold values from -6 to 6
- timesteps: int32 [8, 1], P('hd'), may hold values from 0 to 999
- step: int32 [1], replicated, may hold values from 1 to 20
- query_weight: bfloat16 [320, 320], replicated, may hold values from -0.3125 to 0.3125
- key_weight: bfloat16 [768, 320], replicated, may hold values from -0.21875 to 0.21875
- value_weight: bfloat16 [768, 320], replicated, may hold values from -0.21875 to 0.21875
- out_weight: bfloat16 [320, 320], replicated, may hold values from -1 to 1
- pred_weight: bfloat16 [320, 4], replicated, may hold values from -0.3125 to 0.3125
- master: float32 [1578240], P(('sp', 'hd')), as said below
- first_moment: float32 [1578240], P(('sp', 'hd')), may hold values from -0.0048828125 to 0.0048828125
- second_moment: float32 [1578240], P(('sp', 'hd')), may hold values from 9.536743e-08 to 3.8146973e-07
Outputs:
- loss: float32 [], replicated
- new_master: float32 [1578240], P(('sp', 'hd'))
- new_first: float32 [1578240], P(('sp', 'hd'))
- new_second: float32 [1578240], P(('sp', 'hd'))
The draws below stay inside these ranges and needn't reach their ends.
Inputs may be any that keep to these rules, and one draw needn't show every extreme that they name: `master`: adapter parameters in the stated order.
All inputs are finite; a program needn't handle non-finite values.
Results may differ from the reference program's by a relative error of at most 0.024.
Values may be sent and summed in bfloat16 or wider, within the bound.
No kernel may reach another device: no remote copies, remote signals or barrier semaphores. Data moves between devices by JAX's collectives and lax.ppermute only.
A program may use at most 64 MiB of HBM per device.

```python
import math
import jax
import jax.numpy as jnp
from jax import lax

C = 320
CIN = 192
CTX = 768
HEADS = 8
HDIM = 40
CTXLEN = 77
OUTC = 4
H = 64
W = 64
STACK = 1
CANVASES = 8
IMG = 8
NPAR = 1578240


def draw_master(key, part):
    key_in, key_one, key_two, key_bias, key_gain = jax.random.split(key, 5)
    w_in = jax.random.normal(key_in, (9 * CIN * C,), jnp.float32) / (9 * CIN) ** 0.5
    w_one = jax.random.normal(key_one, (9 * C * C,), jnp.float32) / (9 * C) ** 0.5
    w_two = jax.random.normal(key_two, (C * C,), jnp.float32) / C ** 0.5
    biases = 0.3 * jax.random.normal(key_bias, (3 * C,), jnp.float32)
    inject = jnp.exp(jax.random.uniform(key_gain, (C,), jnp.float32, -0.7, 0.7))
    return jnp.concatenate([w_in, w_one, w_two, biases, inject])


def with_ends(result, rng, smallest, high):
    extent = result.shape
    spot = [jax.random.randint(jax.random.fold_in(rng, axis), (), 0, extent[axis]) for axis in range(len(extent))]
    result = result.at[tuple(spot)].set(smallest)
    longest = extent.index(max(extent))
    spot[longest] = (spot[longest] + 1) % extent[longest]
    return result.at[tuple(spot)].set(high)


def level_of(rng, shape, cuts, least, high):
    factor_of = 1.0
    for dim, blocks in cuts:
        heights = jax.random.uniform(jax.random.fold_in(jax.random.fold_in(rng, 6), dim), (blocks,), jnp.float32, least / len(cuts), high / len(cuts))
        factor_of = factor_of * jnp.repeat(jnp.exp(heights), shape[dim] // blocks).reshape((-1,) + (1,) * (len(shape) - 1 - dim))
    return factor_of


def centred(own_key, dims, spread, bound, cuts=(), kind=jnp.bfloat16):
    values = jax.random.normal(own_key, dims, jnp.float32) * spread
    if len(cuts) > 0:
        values = level_of(own_key, dims, cuts, -0.22, 0.18) * values
    return jnp.clip(values, min=-bound, max=bound).astype(kind)


def setup_inputs(seed: int = 0) -> dict:
    seeds = jax.random.split(jax.random.key(seed), 15)
    cond = centred(seeds[0], (CANVASES, STACK * H, W, CIN), 1.0, 6.0, ((0, 4), (1, 8)))
    resid = centred(seeds[1], (CANVASES, STACK * H, W, C), 1.0, 6.0, ((0, 4), (1, 8)))
    context = centred(seeds[2], (CANVASES, STACK, CTXLEN, CTX), 1.0, 6.0, ((0, 4),))
    noise = centred(seeds[3], (CANVASES, STACK * H, W, OUTC), 1.0, 6.0, ((0, 4), (1, 8)), jnp.float32)
    timesteps = with_ends(jax.random.randint(seeds[4], (CANVASES, STACK), 0, 1000), jax.random.fold_in(seeds[4], 1), 0, 999).astype(jnp.int32)
    step = jax.random.randint(seeds[5], (1,), 1, 21).astype(jnp.int32)
    query_weight = centred(seeds[6], (C, C), C ** -0.5, 0.3125)
    key_weight = centred(seeds[7], (CTX, C), CTX ** -0.5, 0.21875)
    value_weight = centred(seeds[8], (CTX, C), CTX ** -0.5, 0.21875)
    out_weight = centred(seeds[9], (C, C), (C // 8) ** -0.5, 1.0)
    pred_weight = centred(seeds[10], (C, OUTC), C ** -0.5, 0.3125)
    master = draw_master(jax.random.fold_in(seeds[14], 71), 0)
    first_moment = centred(seeds[12], (NPAR,), (1.0 / (C * IMG * H * W) ** 0.5), 0.0048828125, ((0, 32),), jnp.float32)
    second_moment = jnp.clip(jnp.exp(math.log(3.814697322468419e-07) - 1.3862944 * jax.random.uniform(seeds[13], (NPAR,), jnp.float32) ** level_of(seeds[13], (NPAR,), ((0, 32),), -0.2, 0.2)), 9.536743306171047e-08, 3.814697322468419e-07)
    return dict(cond=cond, resid=resid, context=context, noise=noise, timesteps=timesteps, step=step, query_weight=query_weight, key_weight=key_weight, value_weight=value_weight, out_weight=out_weight, pred_weight=pred_weight, master=master, first_moment=first_moment, second_moment=second_moment)


@jax.custom_vjp
def low(v):
    return lax.optimization_barrier(v.astype(jnp.bfloat16)).astype(jnp.float32)

@jax.custom_vjp
def low_back(v):
    return v

def low_keep(v):
    return (low(v), None)

def low_pass(kept, grad):
    return (grad,)

def back_keep(v):
    return (v, None)

def back_low(kept, grad):
    return (low(grad),)
low.defvjp(low_keep, low_pass)
low_back.defvjp(back_keep, back_low)
HIGH = lax.Precision.HIGHEST
EPS_NORM = 1e-05
RATE = 0.05
DECAY = 0.01
BETA_ONE = 0.5
BETA_TWO = 0.5
EPS_ADAM = 1e-08
SNR_CAP = 5.0

def snr_weights(timesteps):
    beta_sched = jnp.linspace(0.00085 ** 0.5, 0.012 ** 0.5, 1000, dtype=jnp.float32) ** 2
    alpha_bar = jnp.exp(jnp.cumsum(jnp.log(1.0 - beta_sched)))
    snr_value = alpha_bar / (1.0 - alpha_bar)
    lookup = jnp.minimum(snr_value, SNR_CAP) / snr_value
    hit_table = timesteps[:, None] == jnp.arange(1000, dtype=jnp.int32)[None, :]
    return lax.optimization_barrier(jnp.sum(jnp.where(hit_table, lookup[None, :], 0.0), axis=1))

def unpack(gathered):
    n_in = 9 * CIN * C
    n_one = 9 * C * C
    n_two = C * C
    w_in = gathered[:n_in].reshape(3, 3, CIN, C)
    w_one = gathered[n_in:n_in + n_one].reshape(3, 3, C, C)
    w_two = gathered[n_in + n_one:n_in + n_one + n_two].reshape(C, C)
    trailing = gathered[n_in + n_one + n_two:].reshape(4, C)
    return (w_in, w_one, w_two, trailing[0], trailing[1], trailing[2], trailing[3])

def conv_same(inputs, kernel):
    return lax.conv_general_dilated(inputs, kernel, (1, 1), 'SAME', dimension_numbers=('NHWC', 'HWIO', 'NHWC'), precision=HIGH)

def forward(params, cond, resid, context, noise, weights, query_weight, key_weight, value_weight, out_weight, pred_weight):
    w_in, w_one, w_two, b_in, b_one, b_two, inject = unpack(low(params))
    a_one = low_back(conv_same(cond, w_in) + b_in)
    pre_relu = low_back(conv_same(low(a_one), w_one) + b_one)
    relu_low = low(jnp.where(pre_relu > 0, pre_relu, 0.0))
    branch = low_back(jnp.einsum('bhwc,cd->bhwd', relu_low, w_two, precision=HIGH) + b_two)
    feature = branch + a_one
    norm_scale = lax.rsqrt(jnp.sum(feature * feature) / (IMG * H * W * C) + EPS_NORM)
    injected = resid + inject * (feature * norm_scale)
    query = low(low_back(jnp.einsum('bhwc,cd->bhwd', low(injected), query_weight, precision=HIGH)))
    key_low = low(jnp.einsum('blc,cd->bld', context, key_weight, precision=HIGH))
    value_low = low(jnp.einsum('blc,cd->bld', context, value_weight, precision=HIGH))
    q_heads = query.reshape(IMG, H * W, HEADS, HDIM)
    k_heads = key_low.reshape(IMG, CTXLEN, HEADS, HDIM)
    v_heads = value_low.reshape(IMG, CTXLEN, HEADS, HDIM)
    scores = low_back(jnp.einsum('bphd,bkhd->bhpk', q_heads, k_heads, precision=HIGH) * HDIM ** (-0.5))
    attn = jax.nn.softmax(scores, axis=-1)
    mixed = low(low_back(jnp.einsum('bhpk,bkhd->bphd', low(attn), v_heads, precision=HIGH))).reshape(IMG, H, W, C)
    after_attn = injected + low_back(jnp.einsum('bhwc,cd->bhwd', mixed, out_weight, precision=HIGH))
    pred = low_back(jnp.einsum('bhwc,cd->bhwd', low(after_attn), pred_weight, precision=HIGH))
    error_term = pred - noise
    per_image = lax.optimization_barrier(jnp.mean(error_term * error_term, axis=(1, 2, 3)))
    return jnp.sum(weights * per_image) / jnp.sum(weights)

def reference(cond, resid, context, noise, timesteps, step, query_weight, key_weight, value_weight, out_weight, pred_weight, master, first_moment, second_moment):
    weights = snr_weights(timesteps.reshape(IMG))
    inputs = [cond.reshape(IMG, H, W, CIN).astype(jnp.float32), resid.reshape(IMG, H, W, C).astype(jnp.float32), context.reshape(IMG, CTXLEN, CTX).astype(jnp.float32), noise.reshape(IMG, H, W, OUTC).astype(jnp.float32), weights, query_weight.astype(jnp.float32), key_weight.astype(jnp.float32), value_weight.astype(jnp.float32), out_weight.astype(jnp.float32), pred_weight.astype(jnp.float32)]

    def loss_of(params):
        return forward(params, *inputs)
    loss, pullback = jax.vjp(loss_of, master)
    grad_flat, = pullback(jnp.ones_like(loss))
    steps_done = step[0].astype(jnp.float32)
    first_new = BETA_ONE * first_moment + (1.0 - BETA_ONE) * grad_flat
    second_new = BETA_TWO * second_moment + (1.0 - BETA_TWO) * grad_flat * grad_flat
    first_hat = first_new / (1.0 - BETA_ONE ** steps_done)
    second_hat = second_new / (1.0 - BETA_TWO ** steps_done)
    new_master = master - RATE * (first_hat / (jnp.sqrt(second_hat) + EPS_ADAM) + DECAY * master)
    return (loss, new_master, first_new, second_new)
```

```python
import functools

import jax
import jax.numpy as jnp
from jax import lax
from jax.experimental import pallas as pl
from jax.experimental.pallas import tpu as pltpu
from jax.sharding import PartitionSpec as P

HDIM = 40
LANES = 128
EPS_NORM = 1e-05
RATE = 0.05
DECAY = 0.01
BETA_ONE = 0.5
BETA_TWO = 0.5
EPS_ADAM = 1e-08
SNR_CAP = 5.0
VMEM = pltpu.VMEM
BF = jnp.bfloat16
F32 = jnp.float32


def mm(a, b):
    return jnp.dot(a, b, preferred_element_type=F32)


def mm_nt(a, b):
    return lax.dot_general(a, b, (((1,), (1,)), ((), ())), preferred_element_type=F32)


def mm_tn(a, b):
    return lax.dot_general(a, b, (((0,), (0,)), ((), ())), preferred_element_type=F32)


def call(kernel, outs, ins, scratch=(), smem=(), flops=0, limit=56):
    specs = [
        pl.BlockSpec(memory_space=pltpu.SMEM if i in smem else VMEM) for i in range(len(ins))
    ]
    return pl.pallas_call(
        kernel,
        out_shape=[jax.ShapeDtypeStruct(s, d) for s, d in outs],
        in_specs=specs,
        out_specs=[pl.BlockSpec(memory_space=VMEM) for _ in outs],
        scratch_shapes=list(scratch),
        compiler_params=pltpu.CompilerParams(vmem_limit_bytes=limit * 1024 * 1024),
        cost_estimate=pl.CostEstimate(flops=flops, bytes_accessed=8 << 20, transcendentals=0),
    )(*ins)


class Plan:
    def __init__(self, sp, hd, length, channels):
        self.sp, self.hd, self.count = sp, hd, sp * hd
        self.length, self.channels = length, channels
        self.start = [length * i // channels for i in range(self.count)]
        need = max(
            -(-(length * i % channels + length) // channels) for i in range(self.count)
        )
        self.rows = -(-need // 32) * 32
        self.packed = self.rows * channels // LANES
        self.part_a = -(-self.packed // 32) * 16
        self.part_b = self.packed - self.part_a
        self.table = -(-(self.start[-1] + self.rows) // 8) * 8
        self.nz, self.nx = max(sp // 2, 1), min(sp, 2)
        self.ny, self.nk = max(hd // 2, 1), min(hd, 2)
        self.group_z = ("sp", sp, self.nx, self.nz)
        self.group_x = ("sp", sp, 1, self.nx)
        self.group_y = ("hd", hd, self.nk, self.ny)
        self.group_k = ("hd", hd, 1, self.nk)
        self.half = self.count // self.nk

    def place(self, owner, me):
        off = owner ^ me
        off_sp, off_hd = off // self.hd, off % self.hd
        z, x = off_sp // self.nx, off_sp % self.nx
        y, k = off_hd // self.nk, off_hd % self.nk
        return k, (y * self.nx + x) * self.nz + z, (x * self.ny + y) * self.nz + z


def swap(value, group, step):
    axis, count, stride, _ = group
    return lax.ppermute(value, axis, [(i, i ^ (step * stride)) for i in range(count)])


def spread(block, group):
    return jnp.concatenate([block] + [swap(block, group, e) for e in range(1, group[3])], axis=0)


def collect(total, group):
    size = total.shape[0] // group[3]
    out = total[:size]
    for e in range(1, group[3]):
        out = out + swap(total[e * size : (e + 1) * size].astype(BF), group, e).astype(F32)
    return out


def pack_rows(table):
    rows = table.shape[0]
    tail = table[:, 2 * LANES :]
    tail = jnp.concatenate([tail[: rows // 2], tail[rows // 2 :]], axis=1)
    return jnp.concatenate([table[:, :LANES], table[:, LANES : 2 * LANES], tail], axis=0)


def unpack_rows(packed, rows):
    tail = packed[2 * rows :]
    half = tail.shape[1] // 2
    tail = jnp.concatenate([tail[:, :half], tail[:, half:]], axis=0)
    return jnp.concatenate([packed[:rows], packed[rows : 2 * rows], tail], axis=1)


def gather_parameters(plan, master):
    me = lax.axis_index("sp") * plan.hd + lax.axis_index("hd")
    shift = lax.rem(me * plan.length, plan.channels)
    flat = jnp.zeros((plan.rows * plan.channels,), F32)
    flat = lax.dynamic_update_slice(flat, master, (shift,))
    packed = pack_rows(flat.reshape(plan.rows, plan.channels).astype(BF))[None]
    part_a, part_b = packed[:, : plan.part_a], packed[:, plan.part_a :]
    for group_a, group_b in (
        (plan.group_z, plan.group_z),
        (plan.group_x, plan.group_y),
        (plan.group_y, plan.group_x),
    ):
        part_a, part_b = spread(part_a, group_a), spread(part_b, group_b)
    if plan.nk == 1:
        return part_a, part_a, part_b, part_b
    return part_a, swap(part_a, plan.group_k, 1), part_b, swap(part_b, plan.group_k, 1)


def scatter_gradient(plan, keep, send):
    total = keep
    if plan.nk > 1:
        total = keep + swap(send, plan.group_k, 1).astype(F32)
    part_a, part_b = total[:, : plan.part_a], total[:, plan.part_a :]
    for group_a, group_b in (
        (plan.group_y, plan.group_x),
        (plan.group_x, plan.group_y),
        (plan.group_z, plan.group_z),
    ):
        part_a, part_b = collect(part_a, group_a), collect(part_b, group_b)
    packed = jnp.concatenate([part_a[0], part_b[0]], axis=0)
    flat = unpack_rows(packed, plan.rows).reshape(-1)
    me = lax.axis_index("sp") * plan.hd + lax.axis_index("hd")
    shift = lax.rem(me * plan.length, plan.channels)
    return lax.dynamic_slice(flat, (shift,), (plan.length,))


def three_columns(values, cols):
    tokens = values.shape[0]
    col = lax.broadcasted_iota(jnp.int32, values.shape, 0) % cols
    left = jnp.where(col == 0, 0.0, pltpu.roll(values, 1, 0))
    right = jnp.where(col == cols - 1, 0.0, pltpu.roll(values, tokens - 1, 0))
    return jnp.concatenate([left, values, right], axis=1).astype(BF)


def lane_pick(row, lane):
    ids = lax.broadcasted_iota(jnp.int32, row.shape, 1)
    return jnp.sum(jnp.where(ids == lane, row, 0.0))


def lane_row(pairs):
    ids = lax.broadcasted_iota(jnp.int32, (1, LANES), 1)
    row = jnp.zeros((1, LANES), F32)
    for lane, value in pairs:
        row = jnp.where(ids == lane, value, row)
    return row


def prepare_kernel(cols, cond, low, high, context, wk, wv, c3, c3t, kbd, kbdt, vbd, vbdt):
    images, tokens, in_chan = cond.shape
    words = context.shape[1]
    channels = wk.shape[1]
    heads = channels // HDIM
    kept = 3 * in_chan
    for i in range(images):
        wide = jnp.concatenate([low[i], cond[i], high[i]], axis=0).astype(F32)
        c3[i] = three_columns(wide, cols)
        for dy in range(3):
            part = c3[i, (1 + dy) * cols : (1 + dy) * cols + tokens]
            c3t[dy * kept : (dy + 1) * kept, i * tokens : (i + 1) * tokens] = part.T
        pad = jnp.zeros((LANES - words, channels), F32)
        key = jnp.concatenate([mm(context[i], wk[...]), pad], axis=0)
        value = jnp.concatenate([mm(context[i], wv[...]), pad], axis=0)
        for source, tall, flat in ((key, kbdt, kbd), (value, vbd, vbdt)):
            turned = source.T
            col_head = lax.broadcasted_iota(jnp.int32, source.shape, 1) // HDIM
            row_head = lax.broadcasted_iota(jnp.int32, turned.shape, 0) // HDIM
            for h in range(heads):
                span = slice(h * LANES, (h + 1) * LANES)
                tall[i, span, :] = jnp.where(col_head == h, source, 0.0).astype(BF)
                flat[i, :, span] = jnp.where(row_head == h, turned, 0.0).astype(BF)


def forward_kernel(
    plan, cols, place, snr, own_a, other_a, own_b, other_b, c3,
    weights, trailing, feature, relu_low, x3, payload, table,
):
    me, first, last = place[0], place[1], place[2]
    rows, split = plan.rows, plan.part_a
    for i in range(plan.count):
        k, at_a, at_b = plan.place(i, me)
        own = jnp.full((1, 1), k, jnp.int32) == 0
        a = jnp.where(own, own_a[at_a].astype(F32), other_a[at_a].astype(F32))
        b = jnp.where(own, own_b[at_b].astype(F32), other_b[at_b].astype(F32))
        begin = plan.start[i]
        old = table[begin : begin + 1, :] if i > 0 else None
        table[begin : begin + rows, :LANES] = a[:rows]
        table[begin : begin + rows, LANES : 2 * LANES] = jnp.concatenate(
            [a[rows:], b[: 2 * rows - split]], axis=0
        )
        tail = b[2 * rows - split :]
        table[begin : begin + rows // 2, 2 * LANES :] = tail[:, : LANES // 2]
        table[begin + rows // 2 : begin + rows, 2 * LANES :] = tail[:, LANES // 2 :]
        if i > 0:
            table[begin : begin + 1, :] += old
    count = weights.shape[0]
    weights[...] = table[:count].astype(BF)
    trailing[...] = jnp.concatenate(
        [table[count : count + 4], jnp.zeros((4, table.shape[1]), F32)], axis=0
    )
    images, wide, kept_in = c3.shape
    channels = table.shape[1]
    tokens = wide - 4 * cols
    kept = 3 * channels
    base_one = 3 * kept_in
    base_two = base_one + 3 * kept
    b_in, b_one, b_two = trailing[0:1], trailing[1:2], trailing[2:3]
    square = jnp.zeros((1, 1), F32)
    for i in range(images):
        more = tokens + 2 * cols
        a_one = b_in + sum(
            mm(c3[i, dy * cols : dy * cols + more], weights[dy * kept_in : (dy + 1) * kept_in])
            for dy in range(3)
        )
        row = lax.broadcasted_iota(jnp.int32, a_one.shape, 0) // cols
        outside = ((row == 0) & (first == 1)) | ((row == tokens // cols + 1) & (last == 1))
        a_low = jnp.where(outside, 0.0, a_one).astype(BF).astype(F32)
        x3[i] = three_columns(a_low, cols)
        pre_relu = b_one + sum(
            mm(
                x3[i, dy * cols : dy * cols + tokens],
                weights[base_one + dy * kept : base_one + (dy + 1) * kept],
            )
            for dy in range(3)
        )
        relu = jnp.maximum(pre_relu, 0.0).astype(BF)
        out = mm(relu, weights[base_two : base_two + channels]) + b_two
        out = out + a_one[cols : cols + tokens]
        span = slice(i * tokens, (i + 1) * tokens)
        relu_low[span] = relu
        feature[span] = out
        square = square + jnp.sum(out * out)
    total = snr[0]
    for i in range(1, images):
        total = total + snr[i]
    line = lane_row([(0, square), (1, total)])
    payload[...] = jnp.broadcast_to(line[None], payload.shape)


def turn_kernel(cols, x3, weights, x3t, w1t):
    images, wide, kept = x3.shape
    tokens = wide - 2 * cols
    channels = kept // 3
    base_one = weights.shape[0] - channels - 3 * kept
    for dy in range(3):
        for i in range(images):
            part = x3[i, dy * cols : dy * cols + tokens]
            x3t[dy * kept : (dy + 1) * kept, i * tokens : (i + 1) * tokens] = part.T
        for dx in range(3):
            begin = base_one + ((2 - dy) * 3 + 2 - dx) * channels
            tap = weights[begin : begin + channels].astype(F32)
            at = (dy * 3 + dx) * channels
            w1t[at : at + channels] = tap.T.astype(BF)


def norm_of(line, elements):
    return lax.rsqrt(jnp.full((1, 1), lane_pick(line, 0) / elements + EPS_NORM, F32))


def attention_kernel(
    plan, sizes, snr, sums, feature, resid, noise, trailing, kbd, kbdt, vbd, vbdt, wq, wo, wp, wpt,
    g_out, u_out, payload,
):
    elements, loss_count, words = sizes
    images, channels, spread_heads = kbd.shape
    tokens = feature.shape[0] // images
    heads = spread_heads // LANES
    line = jnp.sum(sums[...], axis=0)
    scale = norm_of(line, elements)
    denom = lane_pick(line, 1) / plan.sp * loss_count
    inject = trailing[3:4]
    root = HDIM ** (-0.5)
    loss = jnp.zeros((1, 1), F32)
    u = jnp.zeros((1, channels), F32)
    known = lax.broadcasted_iota(jnp.int32, (tokens, LANES), 1) < words
    for i in range(images):
        span = slice(i * tokens, (i + 1) * tokens)
        injected = resid[span].astype(F32) + inject * (feature[span] * scale)
        query = mm(injected.astype(BF), wq[...]).astype(BF)
        scores = mm(query, kbd[i]) * root
        attn = []
        for h in range(heads):
            part = jnp.where(known, scores[:, h * LANES : (h + 1) * LANES], -1e30)
            part = jnp.exp(part - jnp.max(part, axis=1, keepdims=True))
            attn.append(part / jnp.sum(part, axis=1, keepdims=True))
        low = jnp.concatenate([a.astype(BF) for a in attn], axis=1)
        mixed = mm(low, vbd[i]).astype(BF)
        after = injected + mm(mixed, wo[...])
        error = mm(after.astype(BF), wp[...]) - noise[span]
        loss = loss + snr[i] * jnp.sum(error * error)
        g_pred = (2.0 * snr[i] / denom) * error
        g_y = mm(g_pred.astype(BF), wpt[...])
        g_mixed = mm_nt(g_y.astype(BF), wo[...]).astype(BF)
        g_attn = mm(g_mixed, vbdt[i])
        g_scores = []
        for h in range(heads):
            part = g_attn[:, h * LANES : (h + 1) * LANES]
            inner = jnp.sum(attn[h] * part, axis=1, keepdims=True)
            g_scores.append((attn[h] * (part - inner)).astype(BF))
        g_query = (mm(jnp.concatenate(g_scores, axis=1), kbdt[i]) * root).astype(BF)
        g_x = g_y + mm_nt(g_query, wq[...])
        g_out[span] = g_x
        u = u + jnp.sum(g_x * feature[span], axis=0, keepdims=True)
    u_out[...] = jnp.broadcast_to(u, u_out.shape)
    cross = jnp.sum(inject * u)
    payload[...] = jnp.broadcast_to(lane_row([(0, loss / denom), (1, cross)])[None], payload.shape)


def solve_kernel(
    cols, elements, sums, sums_two, g_x, u_in, feature, relu_low, trailing, weights,
    loss, g_f, gz, edge_top, edge_bottom, d_two, d_rows,
):
    images, tokens, channels = gz.shape
    scale = norm_of(jnp.sum(sums[...], axis=0), elements)
    line = jnp.sum(sums_two[...], axis=0)
    loss[...] = jnp.full(loss.shape, lane_pick(line, 0), F32)
    pull = scale * scale * scale * (lane_pick(line, 1) / elements)
    inject = trailing[3:4]
    base_two = weights.shape[0] - channels
    rows = [jnp.zeros((1, channels), F32), jnp.zeros((1, channels), F32)]
    for i in range(images):
        span = slice(i * tokens, (i + 1) * tokens)
        value = scale * (inject * g_x[span]) - feature[span] * pull
        g_f[span] = value
        low = value.astype(BF)
        relu = relu_low[span]
        back = mm_nt(low, weights[base_two:])
        back = jnp.where(relu.astype(F32) > 0, back, 0.0).astype(BF)
        gz[i] = back
        edge_top[i] = back[:cols]
        edge_bottom[i] = back[tokens - cols :]
        part = mm_tn(relu, low)
        d_two[...] = part if i == 0 else d_two[...] + part
        rows[0] = rows[0] + jnp.sum(back.astype(F32), axis=0, keepdims=True)
        rows[1] = rows[1] + jnp.sum(low.astype(F32), axis=0, keepdims=True)
    d_rows[...] = jnp.concatenate(
        rows + [scale * u_in[0:1], jnp.zeros((5, channels), F32)], axis=0
    )


def block_weight_kernel(x3t, gz, d_one):
    images, tokens, channels = gz.shape
    flat = gz[...].reshape(images * tokens, channels)
    size = x3t.shape[0] // 9
    for tap in range(9):
        at = tap * size
        d_one[at : at + size] = mm(x3t[at : at + size], flat)


def input_kernel(
    plan, cols, place, gz, above, below, g_f, w1t, c3t, d_one, d_two, d_rows,
    keep, send, table,
):
    me = place[0]
    images, tokens, channels = gz.shape
    kept = 3 * channels
    n_in, n_one = c3t.shape[0], d_one.shape[0]
    ga = []
    db_in = jnp.zeros((1, channels), F32)
    for i in range(images):
        wide = jnp.concatenate([above[i], gz[i], below[i]], axis=0).astype(F32)
        wide = three_columns(wide, cols)
        total = g_f[i * tokens : (i + 1) * tokens] + sum(
            mm(wide[dy * cols : dy * cols + tokens], w1t[dy * kept : (dy + 1) * kept])
            for dy in range(3)
        )
        ga.append(total.astype(BF))
        db_in = db_in + jnp.sum(ga[i].astype(F32), axis=0, keepdims=True)
    flat = jnp.concatenate(ga, axis=0)
    size = n_in // 9
    for tap in range(9):
        at = tap * size
        table[at : at + size] = mm(c3t[at : at + size], flat)
    table[n_in : n_in + n_one] = d_one[...]
    at = n_in + n_one
    table[at : at + channels] = d_two[...]
    at = at + channels
    table[at : at + 8] = jnp.concatenate(
        [db_in, d_rows[0:3], jnp.zeros((4, channels), F32)], axis=0
    )
    rows, split = plan.rows, plan.part_a
    for i in range(plan.count):
        k, at_a, at_b = plan.place(i, me)
        begin = plan.start[i]
        one = table[begin : begin + rows, :LANES]
        two = table[begin : begin + rows, LANES : 2 * LANES]
        tail = jnp.concatenate(
            [
                table[begin : begin + rows // 2, 2 * LANES :],
                table[begin + rows // 2 : begin + rows, 2 * LANES :],
            ],
            axis=1,
        )
        a = jnp.concatenate([one, two[: split - rows]], axis=0)
        b = jnp.concatenate([two[split - rows :], tail], axis=0)

        @pl.when(k == 0)
        def _():
            keep[at_a, :split] = a
            keep[at_b, split:] = b

        @pl.when(k != 0)
        def _():
            send[at_a, :split] = a.astype(BF)
            send[at_b, split:] = b.astype(BF)


def snr_weights(timesteps):
    beta_sched = jnp.linspace(0.00085**0.5, 0.012**0.5, 1000, dtype=F32) ** 2
    alpha_bar = jnp.exp(jnp.cumsum(jnp.log(1.0 - beta_sched)))
    snr_value = alpha_bar / (1.0 - alpha_bar)
    lookup = jnp.minimum(snr_value, SNR_CAP) / snr_value
    hit_table = timesteps[:, None] == jnp.arange(1000, dtype=jnp.int32)[None, :]
    return jnp.sum(jnp.where(hit_table, lookup[None, :], 0.0), axis=1)


def shift_rows(value, step):
    count = lax.axis_size("sp")
    pairs = [(i, i + step) for i in range(count) if 0 <= i + step < count]
    return lax.ppermute(value, "sp", pairs)


def everywhere(payload):
    return lax.all_to_all(payload, ("sp", "hd"), 0, 0, tiled=True)


def body(
    cond, resid, context, noise, timesteps, step, query_weight, key_weight, value_weight,
    out_weight, pred_weight, master, first_moment, second_moment,
):
    images, row_count, cols, in_chan = cond.shape
    channels = resid.shape[-1]
    out_chan = noise.shape[-1]
    words = context.shape[2]
    tokens = row_count * cols
    all_tokens = images * tokens
    sp, hd = lax.axis_size("sp"), lax.axis_size("hd")
    plan = Plan(sp, hd, master.shape[0], channels)
    height = row_count * sp
    elements = images * hd * height * cols * channels
    heads = channels // HDIM
    n_in, n_one, n_two = 9 * in_chan, 9 * channels, channels
    at_sp = lax.axis_index("sp")
    place = jnp.stack(
        [
            at_sp * hd + lax.axis_index("hd"),
            (at_sp == 0).astype(jnp.int32),
            (at_sp == sp - 1).astype(jnp.int32),
        ]
    )
    gathered = gather_parameters(plan, master)

    low = shift_rows(cond[:, row_count - 2 :], 1).reshape(images, 2 * cols, in_chan)
    high = shift_rows(cond[:, :2], -1).reshape(images, 2 * cols, in_chan)
    snr = snr_weights(timesteps.reshape(-1))
    c3, c3t, kbd, kbdt, vbd, vbdt = call(
        functools.partial(prepare_kernel, cols),
        [
            ((images, tokens + 4 * cols, 3 * in_chan), BF),
            ((n_in, all_tokens), BF),
            ((images, channels, heads * LANES), BF),
            ((images, heads * LANES, channels), BF),
            ((images, heads * LANES, channels), BF),
            ((images, channels, heads * LANES), BF),
        ],
        [
            cond.reshape(images, tokens, in_chan), low, high,
            context.reshape(images, words, -1), key_weight, value_weight,
        ],
    )
    weights, trailing, feature, relu_low, x3, payload = call(
        functools.partial(forward_kernel, plan, cols),
        [
            ((n_in + n_one + n_two, channels), BF),
            ((8, channels), F32),
            ((all_tokens, channels), F32),
            ((all_tokens, channels), BF),
            ((images, tokens + 2 * cols, 3 * channels), BF),
            ((plan.count, 1, LANES), F32),
        ],
        [place, snr, *gathered, c3],
        scratch=[VMEM((plan.table, channels), F32)],
        smem=(0, 1),
        flops=4 << 30,
    )
    sums = everywhere(payload)
    x3t, w1t = call(
        functools.partial(turn_kernel, cols),
        [((n_one, all_tokens), BF), ((n_one, channels), BF)],
        [x3, weights],
    )
    flat_noise = noise.reshape(all_tokens, out_chan)
    flat_noise = jnp.pad(flat_noise, ((0, 0), (0, LANES - out_chan)))
    wide_pred = jnp.pad(pred_weight, ((0, 0), (0, LANES - out_chan)))
    g_x, u, payload = call(
        functools.partial(
            attention_kernel, plan, (elements, height * cols * out_chan, words)
        ),
        [
            ((all_tokens, channels), F32),
            ((8, channels), F32),
            ((plan.count, 1, LANES), F32),
        ],
        [
            snr, sums, feature, resid.reshape(all_tokens, channels), flat_noise, trailing,
            kbd, kbdt, vbd, vbdt, query_weight, out_weight, wide_pred, wide_pred.T,
        ],
        smem=(0,),
        flops=4 << 30,
    )
    sums_two = everywhere(payload)
    loss, g_f, gz, edge_top, edge_bottom, d_two, d_rows = call(
        functools.partial(solve_kernel, cols, elements),
        [
            ((8, LANES), F32),
            ((all_tokens, channels), F32),
            ((images, tokens, channels), BF),
            ((images, cols, channels), BF),
            ((images, cols, channels), BF),
            ((channels, channels), F32),
            ((8, channels), F32),
        ],
        [sums, sums_two, g_x, u, feature, relu_low, trailing, weights],
    )
    above = shift_rows(edge_bottom, 1)
    below = shift_rows(edge_top, -1)
    (d_one,) = call(
        block_weight_kernel, [((n_one, channels), F32)], [x3t, gz], flops=2 << 30
    )
    keep, send = call(
        functools.partial(input_kernel, plan, cols),
        [
            ((plan.half, plan.packed, LANES), F32),
            ((plan.half, plan.packed, LANES), BF),
        ],
        [place, gz, above, below, g_f, w1t, c3t, d_one, d_two, d_rows],
        scratch=[VMEM((plan.table, channels), F32)],
        smem=(0,),
        flops=4 << 30,
    )
    grad_share = scatter_gradient(plan, keep, send)
    steps_done = step[0].astype(F32)
    first_new = BETA_ONE * first_moment + (1.0 - BETA_ONE) * grad_share
    second_new = BETA_TWO * second_moment + (1.0 - BETA_TWO) * grad_share * grad_share
    first_hat = first_new / (1.0 - BETA_ONE**steps_done)
    second_hat = second_new / (1.0 - BETA_TWO**steps_done)
    new_master = master - RATE * (first_hat / (jnp.sqrt(second_hat) + EPS_ADAM) + DECAY * master)
    return (loss[0, 0], new_master, first_new, second_new)


def solution(mesh):
    shard = P(("sp", "hd"))
    placed = (
        P("hd", "sp", None, None),
        P("hd", "sp", None, None),
        P("hd", None, None, None),
        P("hd", "sp", None, None),
        P("hd", None),
        P(),
        P(),
        P(),
        P(),
        P(),
        P(),
        shard,
        shard,
        shard,
    )
    return jax.shard_map(
        body,
        mesh=mesh,
        in_specs=placed,
        out_specs=(P(), shard, shard, shard),
        check_vma=False,
    )
```

```python
import functools

import jax
import jax.numpy as jnp
import numpy as np
from jax import lax
from jax.experimental import pallas as pl
from jax.experimental.pallas import tpu as pltpu
from jax.sharding import PartitionSpec as P

HDIM = 40
LANES = 128
EPS_NORM = 1e-05
RATE = 0.05
DECAY = 0.01
BETA_ONE = 0.5
BETA_TWO = 0.5
EPS_ADAM = 1e-08
SNR_CAP = 5.0
VMEM, HBM, DMA = pltpu.VMEM, pltpu.HBM, pltpu.SemaphoreType.DMA
BF = jnp.bfloat16
F32 = jnp.float32


def mm(a, b):
    return jnp.dot(a, b, preferred_element_type=F32)


def mm_nt(a, b):
    return lax.dot_general(a, b, (((1,), (1,)), ((), ())), preferred_element_type=F32)


def mm_tn(a, b):
    return lax.dot_general(a, b, (((0,), (0,)), ((), ())), preferred_element_type=F32)


def call(
    kernel, outs, ins, scratch=(), far=(), far_out=(), smem=(), free=(), flops=0, limit=40
):
    def space(i):
        return pltpu.SMEM if i in smem else pl.ANY if i in far else VMEM

    def hold(i, x):
        return x if i in smem or i in free else pltpu.with_memory_space_constraint(x, HBM if i in far else VMEM)

    return pl.pallas_call(
        kernel,
        out_shape=[(HBM if i in far_out else VMEM)(*o) for i, o in enumerate(outs)],
        in_specs=[pl.BlockSpec(memory_space=space(i)) for i in range(len(ins))],
        out_specs=[
            pl.BlockSpec(memory_space=pl.ANY if i in far_out else VMEM) for i in range(len(outs))
        ],
        scratch_shapes=list(scratch),
        compiler_params=pltpu.CompilerParams(vmem_limit_bytes=limit * 1024 * 1024),
        cost_estimate=pl.CostEstimate(flops=flops, bytes_accessed=1 << 20, transcendentals=0),
    )(*[hold(i, x) for i, x in enumerate(ins)])


def start(source, target, sem):
    copy = pltpu.make_async_copy(source, target, sem)
    copy.start()
    return copy


class Plan:
    def __init__(self, sp, hd, length, channels):
        self.sp, self.hd, self.count = sp, hd, sp * hd
        self.length, self.channels = length, channels
        self.start = [length * i // channels for i in range(self.count)]
        need = max(
            -(-(length * i % channels + length) // channels) for i in range(self.count)
        )
        self.rows = -(-need // 32) * 32
        self.packed = self.rows * channels // LANES
        self.part_a = -(-self.packed // 32) * 16
        self.part_b = self.packed - self.part_a
        self.table = -(-(self.start[-1] + self.rows) // 8) * 8
        self.nz, self.nx = max(sp // 2, 1), min(sp, 2)
        self.ny, self.nk = max(hd // 2, 1), min(hd, 2)
        self.group_z = ("sp", sp, self.nx, self.nz)
        self.group_x = ("sp", sp, 1, self.nx)
        self.group_y = ("hd", hd, self.nk, self.ny)
        self.group_k = ("hd", hd, 1, self.nk)
        self.half = self.count // self.nk

    def place(self, owner, me):
        off = owner ^ me
        off_sp, off_hd = off // self.hd, off % self.hd
        z, x = off_sp // self.nx, off_sp % self.nx
        y, k = off_hd // self.nk, off_hd % self.nk
        return k, (y * self.nx + x) * self.nz + z, (x * self.ny + y) * self.nz + z


def swap(value, group, step):
    axis, count, stride, _ = group
    return lax.ppermute(value, axis, [(i, i ^ (step * stride)) for i in range(count)])


def spread(block, group):
    return jnp.concatenate([block] + [swap(block, group, e) for e in range(1, group[3])], axis=0)


def collect(total, group):
    size = total.shape[0] // group[3]
    out = total[:size]
    for e in range(1, group[3]):
        out = out + swap(total[e * size : (e + 1) * size].astype(BF), group, e).astype(F32)
    return out


def pack_rows(table):
    rows = table.shape[0]
    tail = table[:, 2 * LANES :]
    tail = jnp.concatenate([tail[: rows // 2], tail[rows // 2 :]], axis=1)
    return jnp.concatenate([table[:, :LANES], table[:, LANES : 2 * LANES], tail], axis=0)


def unpack_rows(packed, rows):
    tail = packed[2 * rows :]
    half = tail.shape[1] // 2
    tail = jnp.concatenate([tail[:, :half], tail[:, half:]], axis=0)
    return jnp.concatenate([packed[:rows], packed[rows : 2 * rows], tail], axis=1)


def gather_parameters(plan, master, edges, prepare):
    me = lax.axis_index("sp") * plan.hd + lax.axis_index("hd")
    shift = lax.rem(me * plan.length, plan.channels)
    flat = jnp.zeros((plan.rows * plan.channels,), F32)
    flat = lax.dynamic_update_slice(flat, master, (shift,))
    packed = pack_rows(flat.reshape(plan.rows, plan.channels).astype(BF))[None]
    packed = spread(packed, plan.group_z)
    packed, edges = lax.optimization_barrier((packed, edges()))
    part_a, part_b = packed[:, : plan.part_a], packed[:, plan.part_a :]
    part_a, part_b = spread(part_a, plan.group_x), spread(part_b, plan.group_y)
    part_a, part_b = spread(part_a, plan.group_y), spread(part_b, plan.group_x)
    part_a, part_b, ready = lax.optimization_barrier((part_a, part_b, prepare(*edges)))
    if plan.nk == 1:
        return (part_a, part_a, part_b, part_b), ready
    other_a, other_b = swap(part_a, plan.group_k, 1), swap(part_b, plan.group_k, 1)
    return (part_a, other_a, part_b, other_b), ready


def scatter_gradient(plan, keep, send):
    total = keep
    if plan.nk > 1:
        total = keep + swap(send, plan.group_k, 1).astype(F32)
    part_a, part_b = total[:, : plan.part_a], total[:, plan.part_a :]
    for group_a, group_b in (
        (plan.group_y, plan.group_x),
        (plan.group_x, plan.group_y),
    ):
        part_a, part_b = collect(part_a, group_a), collect(part_b, group_b)
    packed = collect(jnp.concatenate([part_a, part_b], axis=1), plan.group_z)[0]
    flat = unpack_rows(packed, plan.rows).reshape(-1)
    me = lax.axis_index("sp") * plan.hd + lax.axis_index("hd")
    shift = lax.rem(me * plan.length, plan.channels)
    return lax.dynamic_slice(flat, (shift,), (plan.length,))


def three_columns(values, cols):
    tokens = values.shape[0]
    col = lax.broadcasted_iota(jnp.int32, values.shape, 0) % cols
    left = jnp.where(col == 0, 0.0, pltpu.roll(values, 1, 0))
    right = jnp.where(col == cols - 1, 0.0, pltpu.roll(values, tokens - 1, 0))
    return jnp.concatenate([left, values, right], axis=1).astype(BF)


def lane_pick(row, lane):
    ids = lax.broadcasted_iota(jnp.int32, row.shape, 1)
    return jnp.sum(jnp.where(ids == lane, row, 0.0))


def lane_row(pairs):
    ids = lax.broadcasted_iota(jnp.int32, (1, LANES), 1)
    row = jnp.zeros((1, LANES), F32)
    for lane, value in pairs:
        row = jnp.where(ids == lane, value, row)
    return row


def prepare_kernel(cols, cond, low, high, context, wk_t, wv_t, c3, k_t, v_t):
    images = cond.shape[0]
    channels, words = wk_t.shape[0], context.shape[1]
    pad = jnp.zeros((channels, LANES - words), F32)
    for i in range(images):
        wide = jnp.concatenate([low[i], cond[i], high[i]], axis=0).astype(F32)
        c3[i] = three_columns(wide, cols)
        for weight, out in ((wk_t, k_t), (wv_t, v_t)):
            part = mm_nt(weight[...], context[i])
            out[i] = jnp.concatenate([part, pad], axis=1).astype(BF)


def unpack_table(plan, me, own_a, other_a, own_b, other_b, table):
    rows, split = plan.rows, plan.part_a
    for i in range(plan.count):
        k, at_a, at_b = plan.place(i, me)
        own = jnp.full((1, 1), k, jnp.int32) == 0
        a = jnp.where(own, own_a[at_a].astype(F32), other_a[at_a].astype(F32))
        b = jnp.where(own, own_b[at_b].astype(F32), other_b[at_b].astype(F32))
        begin = plan.start[i]
        old = table[begin : begin + 1, :] if i > 0 else None
        table[begin : begin + rows, :LANES] = a[:rows]
        table[begin : begin + rows, LANES : 2 * LANES] = jnp.concatenate(
            [a[rows:], b[: 2 * rows - split]], axis=0
        )
        tail = b[2 * rows - split :]
        table[begin : begin + rows // 2, 2 * LANES :] = tail[:, : LANES // 2]
        table[begin + rows // 2 : begin + rows, 2 * LANES :] = tail[:, LANES // 2 :]
        if i > 0:
            table[begin : begin + 1, :] += old


def forward_kernel(
    plan, cols, place, snr, own_a, other_a, own_b, other_b, c3_far,
    weights_far, trailing, feature_far, relu_far, x3_far, payload,
    table, weights, c3, feature, relu_low, x3, sems,
):
    me, first, last = place[0], place[1], place[2]
    images, wide, kept_in = c3.shape
    load = [start(c3_far.at[i], c3.at[i], sems.at[i]) for i in range(images)]
    unpack_table(plan, me, own_a, other_a, own_b, other_b, table)
    count = weights.shape[0]
    weights[...] = table[:count].astype(BF)
    stores = [start(weights, weights_far, sems.at[images])]
    trailing[...] = jnp.concatenate(
        [table[count : count + 4], jnp.zeros((4, table.shape[1]), F32)], axis=0
    )
    channels = table.shape[1]
    tokens = wide - 4 * cols
    kept = 3 * channels
    base_one = 3 * kept_in
    base_two = base_one + 3 * kept
    b_in, b_one, b_two = trailing[0:1], trailing[1:2], trailing[2:3]
    square = jnp.zeros((1, 1), F32)
    for i in range(images):
        more = tokens + 2 * cols
        load[i].wait()
        a_one = b_in + sum(
            mm(c3[i, dy * cols : dy * cols + more], weights[dy * kept_in : (dy + 1) * kept_in])
            for dy in range(3)
        )
        row = lax.broadcasted_iota(jnp.int32, a_one.shape, 0) // cols
        outside = ((row == 0) & (first == 1)) | ((row == tokens // cols + 1) & (last == 1))
        a_low = jnp.where(outside, 0.0, a_one).astype(BF).astype(F32)
        x3[i] = three_columns(a_low, cols)
        stores.append(start(x3.at[i], x3_far.at[i], sems.at[images + 1 + 3 * i]))
        pre_relu = b_one + sum(
            mm(
                x3[i, dy * cols : dy * cols + tokens],
                weights[base_one + dy * kept : base_one + (dy + 1) * kept],
            )
            for dy in range(3)
        )
        relu = jnp.maximum(pre_relu, 0.0).astype(BF)
        relu_low[i] = relu
        stores.append(start(relu_low.at[i], relu_far.at[i], sems.at[images + 2 + 3 * i]))
        out = mm(relu, weights[base_two : base_two + channels]) + b_two
        out = out + a_one[cols : cols + tokens]
        feature[i] = out
        stores.append(start(feature.at[i], feature_far.at[i], sems.at[images + 3 + 3 * i]))
        square = square + jnp.sum(out * out)
    total = snr[0]
    for i in range(1, images):
        total = total + snr[i]
    line = lane_row([(0, square), (1, total)])
    payload[...] = jnp.broadcast_to(line[None], payload.shape)
    for copy in stores:
        copy.wait()


def turn_kernel(taps_from, weights_far, w1t_far, weights, w1t, sems):
    size, channels = weights.shape
    start(weights_far.at[taps_from : taps_from + size], weights, sems.at[0]).wait()
    for row in range(9):
        tap = weights[(8 - row) * channels : (9 - row) * channels].astype(F32)
        w1t[row * channels : (row + 1) * channels] = tap.T.astype(BF)
    start(w1t, w1t_far, sems.at[1]).wait()


def norm_of(line, elements):
    return lax.rsqrt(jnp.full((1, 1), lane_pick(line, 0) / elements + EPS_NORM, F32))


def by_head(left, right, turned):
    span = 2 * LANES
    cut = right.shape[1] - span
    if right.shape[0] != span + LANES // 2 or cut != 6 * LANES:
        return mm_nt(left, right) if turned else mm(left, right)
    if not turned:
        most = mm(left[:, :span], right[:span, :cut])
        return jnp.concatenate([most, mm(left[:, LANES:], right[LANES:, cut:])], axis=1)
    most = mm_nt(left[:, :cut], right[:span, :cut])
    rest = mm_nt(left[:, cut:], right[LANES:, cut:])
    return jnp.concatenate(
        [most[:, :LANES], most[:, LANES:] + rest[:, :LANES], rest[:, LANES:]], axis=1
    )


def attention_kernel(
    plan, sizes, snr, sums, trailing, noise_t, k_t, v_t, wp_t, feature_far, resid_far, wq_far, wo_far,
    g_far, u_out, payload, feature, resid, wq, wo, g_out, kbd, vbd, sems,
):
    elements, loss_count, words = sizes
    images, tokens, channels = feature.shape
    heads = kbd.shape[2] // LANES
    loads = [start(wq_far, wq, sems.at[0]), start(wo_far, wo, sems.at[1])]
    for i in range(images):
        loads.append(start(feature_far.at[i], feature.at[i], sems.at[2 + 3 * i]))
        loads.append(start(resid_far.at[i], resid.at[i], sems.at[3 + 3 * i]))
    line = jnp.sum(sums[...], axis=0)
    scale = norm_of(line, elements)
    denom = lane_pick(line, 1) / plan.sp * loss_count
    inject = trailing[3:4]
    root = HDIM ** (-0.5)
    for i in range(images):
        for source, wide in ((k_t, kbd), (v_t, vbd)):
            row_head = lax.broadcasted_iota(jnp.int32, source.shape[1:], 0) // HDIM
            value = source[i].astype(F32)
            for h in range(heads):
                part = jnp.where(row_head == h, value, 0.0).astype(BF)
                wide[i, :, h * LANES : (h + 1) * LANES] = part
    out_chan, width = noise_t.shape[2:]
    spare = jnp.zeros((16 - out_chan, channels), F32)
    wide_pred = jnp.concatenate([wp_t[...].astype(F32), spare], axis=0).astype(BF)
    loss = jnp.zeros((1, 1), F32)
    u = jnp.zeros((1, channels), F32)
    known = lax.broadcasted_iota(jnp.int32, (tokens, LANES), 1) < words
    stores = []
    for i in range(images):
        for copy in loads[:2] * (i == 0) + loads[2 + 2 * i : 4 + 2 * i]:
            copy.wait()
        value = feature[i]
        injected = resid[i].astype(F32) + inject * (value * scale)
        query = mm(injected.astype(BF), wq[...]).astype(BF)
        scores = by_head(query, kbd[i], False) * root
        attn = []
        for h in range(heads):
            part = jnp.where(known, scores[:, h * LANES : (h + 1) * LANES], -1e30)
            part = jnp.exp(part - jnp.max(part, axis=1, keepdims=True))
            attn.append(part / jnp.sum(part, axis=1, keepdims=True))
        low = jnp.concatenate([a.astype(BF) for a in attn], axis=1)
        mixed = by_head(low, vbd[i], True).astype(BF)
        after = injected + mm(mixed, wo[...])
        pred = mm_nt(wide_pred, after.astype(BF))
        noise = jnp.concatenate([noise_t[i, r] for r in range(tokens // width)], axis=1)
        noise = jnp.concatenate([noise, jnp.zeros((16 - out_chan, tokens), F32)], axis=0)
        error = pred - noise
        loss = loss + snr[i] * jnp.sum(error * error)
        g_pred = (2.0 * snr[i] / denom) * error
        g_y = mm_tn(g_pred.astype(BF), wide_pred)
        g_mixed = mm_nt(g_y.astype(BF), wo[...]).astype(BF)
        g_attn = by_head(g_mixed, vbd[i], False)
        g_scores = []
        for h in range(heads):
            part = g_attn[:, h * LANES : (h + 1) * LANES]
            inner = jnp.sum(attn[h] * part, axis=1, keepdims=True)
            g_scores.append((attn[h] * (part - inner)).astype(BF))
        g_query = (by_head(jnp.concatenate(g_scores, axis=1), kbd[i], True) * root).astype(BF)
        g_x = g_y + mm_nt(g_query, wq[...])
        g_out[i] = g_x
        stores.append(start(g_out.at[i], g_far.at[i], sems.at[4 + 3 * i]))
        u = u + jnp.sum(g_x * value, axis=0, keepdims=True)
    u_out[...] = jnp.broadcast_to(u, u_out.shape)
    cross = jnp.sum(inject * u)
    payload[...] = jnp.broadcast_to(lane_row([(0, loss / denom), (1, cross)])[None], payload.shape)
    for copy in stores:
        copy.wait()


def solve_kernel(
    cols, elements, sums, sums_two, trailing, g_far, feature_far, relu_far, weights_far,
    loss, g_f, gz, edge_top, edge_bottom, g_x, feature, relu, w_two, sems,
):
    images, tokens, channels = gz.shape
    base_two = weights_far.shape[0] - channels
    loads = [start(weights_far.at[base_two : base_two + channels], w_two, sems.at[0])]
    for i in range(images):
        for j, (far, near) in enumerate(((g_far, g_x), (feature_far, feature), (relu_far, relu))):
            loads.append(start(far.at[i], near.at[i], sems.at[1 + 3 * i + j]))
    scale = norm_of(jnp.sum(sums[...], axis=0), elements)
    line = jnp.sum(sums_two[...], axis=0)
    loss[...] = jnp.full(loss.shape, lane_pick(line, 0), F32)
    pull = scale * scale * scale * (lane_pick(line, 1) / elements)
    inject = trailing[3:4]
    for i in range(images):
        for copy in loads[:1] * (i == 0) + loads[1 + 3 * i : 4 + 3 * i]:
            copy.wait()
        value = scale * (inject * g_x[i]) - feature[i] * pull
        g_f[i] = value
        back = mm_nt(value.astype(BF), w_two[...])
        back = jnp.where(relu[i].astype(F32) > 0, back, 0.0).astype(BF)
        gz[i] = back
        edge_top[i] = back[:cols]
        edge_bottom[i] = back[tokens - cols :]


def block_weight_kernel(
    cols, elements, sums, u, gz, g_f, relu_far, x3_far, d_block, d_rows, relu, x3, sems
):
    images, tokens, channels = gz.shape
    kept = 3 * channels
    loads = []
    for i in range(images):
        loads.append(start(relu_far.at[i], relu.at[i], sems.at[2 * i]))
        loads.append(start(x3_far.at[i], x3.at[i], sems.at[2 * i + 1]))
    scale = norm_of(jnp.sum(sums[...], axis=0), elements)
    rows = [jnp.zeros((1, channels), F32), jnp.zeros((1, channels), F32)]
    for i in range(images):
        for copy in loads[2 * i : 2 * i + 2]:
            copy.wait()
        back, low = gz[i], g_f[i].astype(BF)
        spans = [
            (x3[i, dy * cols : dy * cols + tokens], back, dy * kept, kept) for dy in range(3)
        ] + [(relu[i], low, 3 * kept, channels)]
        for left, right, at, size in spans:
            part = mm_tn(left, right)
            d_block[at : at + size] = part if i == 0 else d_block[at : at + size] + part
        rows[0] = rows[0] + jnp.sum(back.astype(F32), axis=0, keepdims=True)
        rows[1] = rows[1] + jnp.sum(low.astype(F32), axis=0, keepdims=True)
    d_rows[...] = jnp.concatenate(rows + [scale * u[0:1], jnp.zeros((5, channels), F32)], axis=0)


def pack_table(plan, me, table, keep, send):
    rows, split = plan.rows, plan.part_a
    for i in range(plan.count):
        k, at_a, at_b = plan.place(i, me)
        begin = plan.start[i]
        one = table[begin : begin + rows, :LANES]
        two = table[begin : begin + rows, LANES : 2 * LANES]
        tail = jnp.concatenate(
            [
                table[begin : begin + rows // 2, 2 * LANES :],
                table[begin + rows // 2 : begin + rows, 2 * LANES :],
            ],
            axis=1,
        )
        a = jnp.concatenate([one, two[: split - rows]], axis=0)
        b = jnp.concatenate([two[split - rows :], tail], axis=0)

        @pl.when(k == 0)
        def _():
            keep[at_a, :split] = a
            keep[at_b, split:] = b

        @pl.when(k != 0)
        def _():
            send[at_a, :split] = a.astype(BF)
            send[at_b, split:] = b.astype(BF)


def input_kernel(
    plan, cols, place, gz, above, below, g_f, d_block, d_rows, w1t_far, c3_far,
    keep, send, table, w1t, c3, sems,
):
    me = place[0]
    images, tokens, channels = gz.shape
    kept, kept_in = 3 * channels, c3.shape[2]
    load = start(w1t_far, w1t, sems.at[0])
    late = start(c3_far, c3, sems.at[1])
    n_in, n_block = 3 * kept_in, d_block.shape[0]
    table[n_in : n_in + n_block] = d_block[...]
    wide = []
    for i in range(images):
        part = jnp.concatenate([above[i], gz[i], below[i]], axis=0).astype(F32)
        wide.append(three_columns(part, cols))
    load.wait()
    db_in = jnp.zeros((1, channels), F32)
    for i in range(images):
        total = g_f[i] + sum(
            mm(wide[i][dy * cols : dy * cols + tokens], w1t[dy * kept : (dy + 1) * kept])
            for dy in range(3)
        )
        low = total.astype(BF)
        db_in = db_in + jnp.sum(low.astype(F32), axis=0, keepdims=True)
        if i == 0:
            late.wait()
        for dy in range(3):
            at = slice(dy * kept_in, (dy + 1) * kept_in)
            part = mm_tn(c3[i, (1 + dy) * cols : (1 + dy) * cols + tokens], low)
            table[at] = part if i == 0 else table[at] + part
    at = n_in + n_block
    table[at : at + 8] = jnp.concatenate(
        [db_in, d_rows[0:3], jnp.zeros((4, channels), F32)], axis=0
    )
    pack_table(plan, me, table, keep, send)


def snr_weights(timesteps):
    beta_sched = np.linspace(0.00085**0.5, 0.012**0.5, 1000, dtype=np.float64) ** 2
    alpha_bar = np.cumprod(1.0 - beta_sched)
    snr_value = alpha_bar / (1.0 - alpha_bar)
    lookup = jnp.asarray(np.minimum(snr_value, SNR_CAP) / snr_value, F32)
    hit_table = timesteps[:, None] == jnp.arange(1000, dtype=jnp.int32)[None, :]
    return jnp.sum(jnp.where(hit_table, lookup[None, :], 0.0), axis=1)


def shift_rows(value, step):
    count = lax.axis_size("sp")
    pairs = [(i, i + step) for i in range(count) if 0 <= i + step < count]
    return lax.ppermute(value, "sp", pairs)


def everywhere(payload):
    return lax.all_to_all(payload, ("sp", "hd"), 0, 0, tiled=True)


def body(
    cond, resid, context, noise, timesteps, step, query_weight, key_weight, value_weight,
    out_weight, pred_weight, master, first_moment, second_moment,
):
    images, row_count, cols, in_chan = cond.shape
    channels = resid.shape[-1]
    out_chan = noise.shape[-1]
    words = context.shape[2]
    tokens = row_count * cols
    all_tokens = images * tokens
    sp, hd = lax.axis_size("sp"), lax.axis_size("hd")
    plan = Plan(sp, hd, master.shape[0], channels)
    height = row_count * sp
    elements = images * hd * height * cols * channels
    heads = channels // HDIM
    n_in, n_one, n_two = 9 * in_chan, 9 * channels, channels
    at_sp = lax.axis_index("sp")
    place = jnp.stack(
        [
            at_sp * hd + lax.axis_index("hd"),
            (at_sp == 0).astype(jnp.int32),
            (at_sp == sp - 1).astype(jnp.int32),
        ]
    )
    snr = snr_weights(timesteps.reshape(-1))
    wide, kept, kept_in = tokens + 2 * cols, 3 * channels, 3 * in_chan

    def edges():
        low = shift_rows(cond[:, row_count - 2 :], 1).reshape(images, 2 * cols, in_chan)
        high = shift_rows(cond[:, :2], -1).reshape(images, 2 * cols, in_chan)
        return low, high

    def prepare(low, high):
        return call(
            functools.partial(prepare_kernel, cols),
            [
                ((images, wide + 2 * cols, kept_in), BF),
                ((images, channels, LANES), BF),
                ((images, channels, LANES), BF),
            ],
            [
                cond.reshape(images, tokens, in_chan), low, high,
                context.reshape(images, words, -1), key_weight.T, value_weight.T,
            ],
            free=(0, 3, 4, 5),
            flops=4 << 30,
        )

    gathered, (c3, k_t, v_t) = gather_parameters(plan, master, edges, prepare)
    line = ((plan.count, 1, LANES), F32)
    per_image = (images, tokens, channels)
    weights, trailing, feature, relu_low, x3, payload = call(
        functools.partial(forward_kernel, plan, cols),
        [
            ((n_in + n_one + n_two, channels), BF),
            ((8, channels), F32),
            (per_image, F32),
            (per_image, BF),
            ((images, wide, kept), BF),
            line,
        ],
        [place, snr, *gathered, c3],
        scratch=[
            VMEM((plan.table, channels), F32),
            VMEM((n_in + n_one + n_two, channels), BF),
            VMEM((images, wide + 2 * cols, kept_in), BF),
            VMEM(per_image, F32),
            VMEM(per_image, BF),
            VMEM((images, wide, kept), BF),
            DMA((1 + 4 * images,)),
        ],
        smem=(0, 1),
        far=(6,),
        far_out=(0, 2, 3, 4),
        flops=4 << 30,
    )
    sums = everywhere(payload)
    (w1t,) = call(
        functools.partial(turn_kernel, n_in),
        [((n_one, channels), BF)],
        [weights],
        scratch=[VMEM((n_one, channels), BF), VMEM((n_one, channels), BF), DMA((2,))],
        far=(0,),
        far_out=(0,),
        flops=2 << 30,
    )
    g_x, u, payload = call(
        functools.partial(
            attention_kernel, plan, (elements, height * cols * out_chan, words)
        ),
        [(per_image, F32), ((8, channels), F32), line],
        [
            snr, sums, trailing, jnp.transpose(noise, (0, 1, 3, 2)), k_t, v_t, pred_weight.T,
            feature, resid.reshape(per_image), query_weight, out_weight,
        ],
        scratch=[
            VMEM(per_image, F32),
            VMEM(per_image, BF),
            VMEM((channels, channels), BF),
            VMEM((channels, channels), BF),
            VMEM(per_image, F32),
            VMEM((images, channels, heads * LANES), BF),
            VMEM((images, channels, heads * LANES), BF),
            DMA((2 + 3 * images,)),
        ],
        smem=(0,),
        far=(7, 8, 9, 10),
        far_out=(0,),
        flops=4 << 30,
    )
    sums_two = everywhere(payload)
    loss, g_f, gz, edge_top, edge_bottom = call(
        functools.partial(solve_kernel, cols, elements),
        [
            ((8, LANES), F32),
            (per_image, F32),
            (per_image, BF),
            ((images, cols, channels), BF),
            ((images, cols, channels), BF),
        ],
        [sums, sums_two, trailing, g_x, feature, relu_low, weights],
        scratch=[
            VMEM(per_image, F32),
            VMEM(per_image, F32),
            VMEM(per_image, BF),
            VMEM((channels, channels), BF),
            DMA((1 + 3 * images,)),
        ],
        far=(3, 4, 5, 6),
        flops=1 << 29,
    )
    above = shift_rows(edge_bottom, 1)
    below = shift_rows(edge_top, -1)
    d_block, d_rows = call(
        functools.partial(block_weight_kernel, cols, elements),
        [((n_one + n_two, channels), F32), ((8, channels), F32)],
        [sums, u, gz, g_f, relu_low, x3],
        scratch=[VMEM(per_image, BF), VMEM((images, wide, kept), BF), DMA((2 * images,))],
        far=(4, 5),
        flops=2 << 30,
    )
    keep, send = call(
        functools.partial(input_kernel, plan, cols),
        [
            ((plan.half, plan.packed, LANES), F32),
            ((plan.half, plan.packed, LANES), BF),
        ],
        [place, gz, above, below, g_f, d_block, d_rows, w1t, c3],
        scratch=[
            VMEM((plan.table, channels), F32),
            VMEM((n_one, channels), BF),
            VMEM((images, wide + 2 * cols, kept_in), BF),
            DMA((2,)),
        ],
        smem=(0,),
        far=(7, 8),
        flops=4 << 30,
    )
    grad_share = scatter_gradient(plan, keep, send)
    steps_done = step[0].astype(F32)
    first_new = BETA_ONE * first_moment + (1.0 - BETA_ONE) * grad_share
    second_new = BETA_TWO * second_moment + (1.0 - BETA_TWO) * grad_share * grad_share
    first_hat = first_new / (1.0 - BETA_ONE**steps_done)
    second_hat = second_new / (1.0 - BETA_TWO**steps_done)
    new_master = master - RATE * (first_hat / (jnp.sqrt(second_hat) + EPS_ADAM) + DECAY * master)
    return (loss[0, 0], new_master, first_new, second_new)


def solution(mesh):
    shard = P(("sp", "hd"))
    placed = (
        P("hd", "sp", None, None),
        P("hd", "sp", None, None),
        P("hd", None, None, None),
        P("hd", "sp", None, None),
        P("hd", None),
        P(),
        P(),
        P(),
        P(),
        P(),
        P(),
        shard,
        shard,
        shard,
    )
    return jax.shard_map(
        body,
        mesh=mesh,
        in_specs=placed,
        out_specs=(P(), shard, shard, shard),
        check_vma=False,
    )
```

```python
import functools

import jax
import jax.numpy as jnp
import numpy as np
from jax import lax
from jax.experimental import pallas as pl
from jax.experimental.pallas import tpu as pltpu
from jax.sharding import PartitionSpec as P

HDIM = 40
LANES = 128
EPS_NORM = 1e-05
RATE = 0.05
DECAY = 0.01
BETA_ONE = 0.5
BETA_TWO = 0.5
EPS_ADAM = 1e-08
SNR_CAP = 5.0
VMEM, HBM, DMA = pltpu.VMEM, pltpu.HBM, pltpu.SemaphoreType.DMA
BF = jnp.bfloat16
F32 = jnp.float32


def mm(a, b):
    return jnp.dot(a, b, preferred_element_type=F32)


def mm_nt(a, b):
    return lax.dot_general(a, b, (((1,), (1,)), ((), ())), preferred_element_type=F32)


def mm_tn(a, b):
    return lax.dot_general(a, b, (((0,), (0,)), ((), ())), preferred_element_type=F32)


def call(
    kernel, outs, ins, scratch=(), far=(), far_out=(), smem=(), free=(), flops=0, limit=40
):
    def space(i):
        return pltpu.SMEM if i in smem else pl.ANY if i in far else VMEM

    def hold(i, x):
        return x if i in smem or i in free else pltpu.with_memory_space_constraint(x, HBM if i in far else VMEM)

    return pl.pallas_call(
        kernel,
        out_shape=[(HBM if i in far_out else VMEM)(*o) for i, o in enumerate(outs)],
        in_specs=[pl.BlockSpec(memory_space=space(i)) for i in range(len(ins))],
        out_specs=[
            pl.BlockSpec(memory_space=pl.ANY if i in far_out else VMEM) for i in range(len(outs))
        ],
        scratch_shapes=list(scratch),
        compiler_params=pltpu.CompilerParams(vmem_limit_bytes=limit * 1024 * 1024),
        cost_estimate=pl.CostEstimate(flops=flops, bytes_accessed=1 << 20, transcendentals=0),
    )(*[hold(i, x) for i, x in enumerate(ins)])


def start(source, target, sem):
    copy = pltpu.make_async_copy(source, target, sem)
    copy.start()
    return copy


class Plan:
    def __init__(self, sp, hd, length, channels):
        self.sp, self.hd, self.count = sp, hd, sp * hd
        self.length, self.channels = length, channels
        self.start = [length * i // channels for i in range(self.count)]
        need = max(
            -(-(length * i % channels + length) // channels) for i in range(self.count)
        )
        self.rows = -(-need // 32) * 32
        self.packed = self.rows * channels // LANES
        self.part_a = -(-self.packed // 32) * 16
        self.part_b = self.packed - self.part_a
        self.table = -(-(self.start[-1] + self.rows) // 8) * 8
        self.nz, self.nx = max(sp // 2, 1), min(sp, 2)
        self.ny, self.nk = max(hd // 2, 1), min(hd, 2)
        self.group_z = ("sp", sp, self.nx, self.nz)
        self.group_x = ("sp", sp, 1, self.nx)
        self.group_y = ("hd", hd, self.nk, self.ny)
        self.group_k = ("hd", hd, 1, self.nk)
        self.half = self.count // self.nk

    def place(self, owner, me):
        off = owner ^ me
        off_sp, off_hd = off // self.hd, off % self.hd
        z, x = off_sp // self.nx, off_sp % self.nx
        y, k = off_hd // self.nk, off_hd % self.nk
        return k, (y * self.nx + x) * self.nz + z, (x * self.ny + y) * self.nz + z


def swap(value, group, step):
    axis, count, stride, _ = group
    return lax.ppermute(value, axis, [(i, i ^ (step * stride)) for i in range(count)])


def spread(block, group):
    return jnp.concatenate([block] + [swap(block, group, e) for e in range(1, group[3])], axis=0)


def collect(total, group):
    size = total.shape[0] // group[3]
    out = total[:size]
    for e in range(1, group[3]):
        out = out + swap(total[e * size : (e + 1) * size].astype(BF), group, e).astype(F32)
    return out


def pack_rows(table):
    rows = table.shape[0]
    tail = table[:, 2 * LANES :]
    tail = jnp.concatenate([tail[: rows // 2], tail[rows // 2 :]], axis=1)
    return jnp.concatenate([table[:, :LANES], table[:, LANES : 2 * LANES], tail], axis=0)


def unpack_rows(packed, rows):
    tail = packed[2 * rows :]
    half = tail.shape[1] // 2
    tail = jnp.concatenate([tail[:, :half], tail[:, half:]], axis=0)
    return jnp.concatenate([packed[:rows], packed[rows : 2 * rows], tail], axis=1)


def gather_parameters(plan, master, edges, prepare):
    me = lax.axis_index("sp") * plan.hd + lax.axis_index("hd")
    shift = lax.rem(me * plan.length, plan.channels)
    total = plan.rows * plan.channels
    flat = jnp.pad(master, (plan.channels, total - plan.length))
    flat = lax.dynamic_slice(flat, (plan.channels - shift,), (total,))
    packed = pack_rows(flat.reshape(plan.rows, plan.channels).astype(BF))[None]
    packed = spread(packed, plan.group_z)
    packed, edges = lax.optimization_barrier((packed, edges()))
    part_a, part_b = packed[:, : plan.part_a], packed[:, plan.part_a :]
    part_a, part_b = spread(part_a, plan.group_x), spread(part_b, plan.group_y)
    part_a, part_b = spread(part_a, plan.group_y), spread(part_b, plan.group_x)
    part_a, part_b, ready = lax.optimization_barrier((part_a, part_b, prepare(*edges)))
    if plan.nk == 1:
        return (part_a, part_a, part_b, part_b), ready
    other_a, other_b = swap(part_a, plan.group_k, 1), swap(part_b, plan.group_k, 1)
    return (part_a, other_a, part_b, other_b), ready


def scatter_gradient(plan, keep, send):
    total = keep[: plan.half].astype(F32)
    if plan.nk > 1:
        total = total + swap(send, plan.group_k, 1)[: plan.half].astype(F32)
    part_a, part_b = total[:, : plan.part_a], total[:, plan.part_a :]
    for group_a, group_b in (
        (plan.group_y, plan.group_x),
        (plan.group_x, plan.group_y),
    ):
        part_a, part_b = collect(part_a, group_a), collect(part_b, group_b)
    packed = collect(jnp.concatenate([part_a, part_b], axis=1), plan.group_z)[0]
    flat = unpack_rows(packed, plan.rows).reshape(-1)
    me = lax.axis_index("sp") * plan.hd + lax.axis_index("hd")
    shift = lax.rem(me * plan.length, plan.channels)
    return lax.dynamic_slice(flat, (shift,), (plan.length,))


def three_columns(values, cols):
    tokens = values.shape[0]
    col = lax.broadcasted_iota(jnp.int32, values.shape, 0) % cols
    left = jnp.where(col == 0, 0.0, pltpu.roll(values, 1, 0))
    right = jnp.where(col == cols - 1, 0.0, pltpu.roll(values, tokens - 1, 0))
    return jnp.concatenate([left, values, right], axis=1).astype(BF)


def lane_pick(row, lane):
    ids = lax.broadcasted_iota(jnp.int32, row.shape, 1)
    return jnp.sum(jnp.where(ids == lane, row, 0.0))


def lane_row(pairs):
    ids = lax.broadcasted_iota(jnp.int32, (1, LANES), 1)
    row = jnp.zeros((1, LANES), F32)
    for lane, value in pairs:
        row = jnp.where(ids == lane, value, row)
    return row


def prepare_kernel(cols, cond, low, high, context, wk_t, wv_t, c3, k_t, v_t):
    images = cond.shape[0]
    channels, words = wk_t.shape[0], context.shape[1]
    pad = jnp.zeros((channels, LANES - words), F32)
    for i in range(images):
        wide = jnp.concatenate([low[i], cond[i], high[i]], axis=0).astype(F32)
        c3[i] = three_columns(wide, cols)
        for weight, out in ((wk_t, k_t), (wv_t, v_t)):
            part = mm_nt(weight[...], context[i])
            out[i] = jnp.concatenate([part, pad], axis=1).astype(BF)


def unpack_table(plan, me, own_a, other_a, own_b, other_b, table, owners):
    rows, split = plan.rows, plan.part_a
    for i in owners:
        k, at_a, at_b = plan.place(i, me)
        own = jnp.full((1, 1), k, jnp.int32) == 0
        a = jnp.where(own, own_a[at_a].astype(F32), other_a[at_a].astype(F32))
        b = jnp.where(own, own_b[at_b].astype(F32), other_b[at_b].astype(F32))
        begin = plan.start[i]
        old = table[begin : begin + 1, :] if i > 0 else None
        table[begin : begin + rows, :LANES] = a[:rows]
        table[begin : begin + rows, LANES : 2 * LANES] = jnp.concatenate(
            [a[rows:], b[: 2 * rows - split]], axis=0
        )
        tail = b[2 * rows - split :]
        table[begin : begin + rows // 2, 2 * LANES :] = tail[:, : LANES // 2]
        table[begin + rows // 2 : begin + rows, 2 * LANES :] = tail[:, LANES // 2 :]
        if i > 0:
            table[begin : begin + 1, :] += old


def forward_kernel(
    plan, cols, place, snr, own_a, other_a, own_b, other_b, c3_far,
    w1t_far, w_two_far, trailing, feature_far, relu_far, x3_far, payload,
    table, weights, w1t, c3, feature, relu_low, x3, sems,
):
    me, first, last = place[0], place[1], place[2]
    images, wide, kept_in = c3.shape
    load = [start(c3_far.at[i], c3.at[i], sems.at[i]) for i in range(images)]
    count, channels = weights.shape
    tokens = wide - 4 * cols
    more = tokens + 2 * cols
    kept = 3 * channels
    n_in = 3 * kept_in
    base_two = n_in + 3 * kept
    blocks = (own_a, other_a, own_b, other_b, table)
    early = [i for i in range(plan.count) if plan.start[i] < n_in]
    unpack_table(plan, me, *blocks, early)
    weights[:n_in] = table[:n_in].astype(BF)
    for copy in load:
        copy.wait()
    a_one = [
        sum(
            mm(c3[i, dy * cols : dy * cols + more], weights[dy * kept_in : (dy + 1) * kept_in])
            for dy in range(3)
        )
        for i in range(images)
    ]
    unpack_table(plan, me, *blocks, range(len(early), plan.count))
    weights[n_in:] = table[n_in:count].astype(BF)
    for row in range(9):
        at = n_in + (8 - row) * channels
        w1t[row * channels : (row + 1) * channels] = table[at : at + channels].T.astype(BF)
    first_store = start(w1t, w1t_far, sems.at[1 + 4 * images])
    stores = [first_store, start(weights.at[base_two : base_two + channels], w_two_far, sems.at[images])]
    trailing[...] = jnp.concatenate([table[count : count + 4], jnp.zeros((4, channels), F32)], axis=0)
    b_in, b_one, b_two = trailing[0:1], trailing[1:2], trailing[2:3]
    square = jnp.zeros((1, 1), F32)
    row = lax.broadcasted_iota(jnp.int32, (more, channels), 0) // cols
    outside = ((row == 0) & (first == 1)) | ((row == tokens // cols + 1) & (last == 1))
    for i in range(images):
        a_one[i] = a_one[i] + b_in
        a_low = jnp.where(outside, 0.0, a_one[i]).astype(BF).astype(F32)
        x3[i] = three_columns(a_low, cols)
        stores.append(start(x3.at[i], x3_far.at[i], sems.at[images + 1 + 3 * i]))
    for i in range(images):
        pre_relu = b_one + sum(
            mm(
                x3[i, dy * cols : dy * cols + tokens],
                weights[n_in + dy * kept : n_in + (dy + 1) * kept],
            )
            for dy in range(3)
        )
        relu = jnp.maximum(pre_relu, 0.0).astype(BF)
        relu_low[i] = relu
        stores.append(start(relu_low.at[i], relu_far.at[i], sems.at[images + 2 + 3 * i]))
        out = mm(relu, weights[base_two : base_two + channels]) + b_two
        out = out + a_one[i][cols : cols + tokens]
        feature[i] = out
        stores.append(start(feature.at[i], feature_far.at[i], sems.at[images + 3 + 3 * i]))
        square = square + jnp.sum(out * out)
    total = snr[0]
    for i in range(1, images):
        total = total + snr[i]
    line = lane_row([(0, square), (1, total)])
    payload[...] = jnp.broadcast_to(line[None], payload.shape)
    for copy in stores:
        copy.wait()


def norm_of(line, elements):
    return lax.rsqrt(jnp.full((1, 1), lane_pick(line, 0) / elements + EPS_NORM, F32))


def by_head(left, right, turned):
    span = 2 * LANES
    cut = right.shape[1] - span
    if right.shape[0] != span + LANES // 2 or cut != 6 * LANES:
        return mm_nt(left, right) if turned else mm(left, right)
    if not turned:
        most = mm(left[:, :span], right[:span, :cut])
        return jnp.concatenate([most, mm(left[:, LANES:], right[LANES:, cut:])], axis=1)
    most = mm_nt(left[:, :cut], right[:span, :cut])
    rest = mm_nt(left[:, cut:], right[LANES:, cut:])
    return jnp.concatenate(
        [most[:, :LANES], most[:, LANES:] + rest[:, :LANES], rest[:, LANES:]], axis=1
    )


def attention_kernel(
    plan, sizes, snr, sums, trailing, noise_t, k_t, v_t, wp_t, feature_far, resid_far, wq_far, wo_far,
    g_far, u_out, payload, feature, resid, wq, wo, g_out, kbd, vbd, sems,
):
    elements, loss_count, words = sizes
    images, tokens, channels = feature.shape
    heads = kbd.shape[2] // LANES
    loads = [start(wq_far, wq, sems.at[0]), start(wo_far, wo, sems.at[1])]
    for i in range(images):
        loads.append(start(feature_far.at[i], feature.at[i], sems.at[2 + 2 * i]))
        loads.append(start(resid_far.at[i], resid.at[i], sems.at[3 + 2 * i]))
    line = jnp.sum(sums[...], axis=0)
    scale = norm_of(line, elements)
    denom = lane_pick(line, 1) / plan.sp * loss_count
    inject = trailing[3:4]
    root = HDIM ** (-0.5)
    for i in range(images):
        for source, wide in ((k_t, kbd), (v_t, vbd)):
            row_head = lax.broadcasted_iota(jnp.int32, source.shape[1:], 0) // HDIM
            value = source[i].astype(F32)
            for h in range(heads):
                part = jnp.where(row_head == h, value, 0.0).astype(BF)
                wide[i, :, h * LANES : (h + 1) * LANES] = part
    out_chan, width = noise_t.shape[2:]
    spare = jnp.zeros((16 - out_chan, channels), F32)
    wide_pred = jnp.concatenate([wp_t[...].astype(F32), spare], axis=0).astype(BF)
    known = lax.broadcasted_iota(jnp.int32, (tokens, LANES), 1) < words
    each = range(images)
    injected, scores = [], []
    for i in each:
        for copy in loads[:2] * (i == 0) + loads[2 + 2 * i : 4 + 2 * i]:
            copy.wait()
        injected.append(resid[i].astype(F32) + inject * (feature[i] * scale))
        query = mm(injected[i].astype(BF), wq[...]).astype(BF)
        scores.append(by_head(query, kbd[i], False))
    attn = []
    for i in each:
        attn.append([])
        for h in range(heads):
            part = jnp.where(known, scores[i][:, h * LANES : (h + 1) * LANES] * root, -1e30)
            part = jnp.exp(part - jnp.max(part, axis=1, keepdims=True))
            attn[i].append(part / jnp.sum(part, axis=1, keepdims=True))
    loss = jnp.zeros((1, 1), F32)
    g_y, g_attn = [], []
    for i in each:
        low = jnp.concatenate([part.astype(BF) for part in attn[i]], axis=1)
        mixed = by_head(low, vbd[i], True).astype(BF)
        after = injected[i] + mm(mixed, wo[...])
        pred = mm_nt(wide_pred, after.astype(BF))
        noise = jnp.concatenate([noise_t[i, r] for r in range(tokens // width)], axis=1)
        noise = jnp.concatenate([noise, jnp.zeros((16 - out_chan, tokens), F32)], axis=0)
        error = pred - noise
        loss = loss + snr[i] * jnp.sum(error * error)
        g_pred = (2.0 * snr[i] / denom) * error
        g_y.append(mm_tn(g_pred.astype(BF), wide_pred))
        g_mixed = mm_nt(g_y[i].astype(BF), wo[...]).astype(BF)
        g_attn.append(by_head(g_mixed, vbd[i], False))
    g_scores = []
    for i in each:
        g_scores.append([])
        for h in range(heads):
            part = g_attn[i][:, h * LANES : (h + 1) * LANES]
            inner = jnp.sum(attn[i][h] * part, axis=1, keepdims=True)
            g_scores[i].append((attn[i][h] * (part - inner)).astype(BF))
    u = jnp.zeros((1, channels), F32)
    stores = []
    for i in each:
        g_query = by_head(jnp.concatenate(g_scores[i], axis=1), kbd[i], True) * root
        g_x = g_y[i] + mm_nt(g_query.astype(BF), wq[...])
        g_out[i] = scale * (inject * g_x)
        stores.append(start(g_out.at[i], g_far.at[i], sems.at[2 + 2 * images + i]))
        u = u + jnp.sum(g_x * feature[i], axis=0, keepdims=True)
    u_out[...] = jnp.broadcast_to(u, u_out.shape)
    cross = jnp.sum(inject * u)
    payload[...] = jnp.broadcast_to(lane_row([(0, loss / denom), (1, cross)])[None], payload.shape)
    for copy in stores:
        copy.wait()


def back_kernel(
    g_far, feature_far, relu_far, w_two_far, by_g, by_feature, g, feature, relu, w_two, sems
):
    images, tokens, channels = by_g.shape
    loads = [start(w_two_far, w_two, sems.at[0])]
    pairs = ((feature_far, feature), (relu_far, relu), (g_far, g))
    for j, (far, near) in enumerate(pairs):
        loads.append(start(far, near, sems.at[1 + j]))
    for copy in loads[:3]:
        copy.wait()
    for i in range(images):
        back = mm_nt(feature[i].astype(BF), w_two[...])
        by_feature[i] = jnp.where(relu[i].astype(F32) > 0, back, 0.0)
    loads[3].wait()
    for i in range(images):
        back = mm_nt(g[i].astype(BF), w_two[...])
        by_g[i] = jnp.where(relu[i].astype(F32) > 0, back, 0.0)


def solve_kernel(
    cols, elements, sums, sums_two, by_g, by_feature, scalars, gz, edge_top, edge_bottom
):
    images, tokens, channels = gz.shape
    scale = norm_of(jnp.sum(sums[...], axis=0), elements)
    line = jnp.sum(sums_two[...], axis=0)
    pull = scale * scale * scale * (lane_pick(line, 1) / elements)
    pairs = [(0, jnp.full((1, 1), lane_pick(line, 0), F32)), (1, pull), (2, scale)]
    scalars[...] = jnp.broadcast_to(lane_row(pairs), scalars.shape)
    for i in range(images):
        back = (by_g[i] - pull * by_feature[i]).astype(BF)
        gz[i] = back
        edge_top[i] = back[:cols]
        edge_bottom[i] = back[tokens - cols :]


def block_weight_kernel(
    cols, scalars, u, gz, x3_far, relu_far, g_far, feature_far,
    d_block, d_rows, g_f, x3, relu, g, feature, sems,
):
    images, tokens, channels = gz.shape
    kept = 3 * channels
    loads = [start(x3_far.at[i], x3.at[i], sems.at[i]) for i in range(images)]
    late = [
        start(far, near, sems.at[images + j])
        for j, (far, near) in enumerate(((relu_far, relu), (g_far, g), (feature_far, feature)))
    ]
    pull, scale = scalars[0:1, 1:2], scalars[0:1, 2:3]
    rows = [jnp.zeros((1, channels), F32), jnp.zeros((1, channels), F32)]
    for i in range(images):
        loads[i].wait()
        for dy in range(3):
            at = slice(dy * kept, (dy + 1) * kept)
            part = mm_tn(x3[i, dy * cols : dy * cols + tokens], gz[i])
            d_block[at] = part if i == 0 else d_block[at] + part
        rows[0] = rows[0] + jnp.sum(gz[i].astype(F32), axis=0, keepdims=True)
    for copy in late:
        copy.wait()
    at = slice(3 * kept, 3 * kept + channels)
    for i in range(images):
        g_f[i] = g[i] - pull * feature[i]
        low = g_f[i].astype(BF)
        part = mm_tn(relu[i], low)
        d_block[at] = part if i == 0 else d_block[at] + part
        rows[1] = rows[1] + jnp.sum(low.astype(F32), axis=0, keepdims=True)
    d_rows[...] = jnp.concatenate(rows + [scale * u[0:1], jnp.zeros((5, channels), F32)], axis=0)


def pack_rows_of(plan, me, i, table, begin, keep, send):
    rows, split = plan.rows, plan.part_a
    k, at_a, at_b = plan.place(i, me)
    half = begin + rows // 2
    one = table[begin : begin + rows, :LANES]
    two = table[begin : begin + rows, LANES : 2 * LANES]
    tail = jnp.concatenate(
        [table[begin:half, 2 * LANES :], table[half : begin + rows, 2 * LANES :]], axis=1
    )
    a = jnp.concatenate([one, two[: split - rows]], axis=0).astype(BF)
    b = jnp.concatenate([two[split - rows :], tail], axis=0).astype(BF)
    for wanted, out in ((0, keep), (1, send)):
        hit = k == wanted
        out[jnp.where(hit, at_a, plan.half), :split] = a
        out[jnp.where(hit, at_b, plan.half), split:] = b


def input_kernel(
    plan, cols, place, gz, above, below, g_f, d_block, d_rows, w1t_far, c3_far,
    keep, send, table, w1t, c3, sems,
):
    me = place[0]
    images, tokens, channels = gz.shape
    kept, kept_in = 3 * channels, c3.shape[2]
    load = start(w1t_far, w1t, sems.at[0])
    late = start(c3_far, c3, sems.at[1])
    n_in, n_block = 3 * kept_in, d_block.shape[0]
    inner = [
        i for i in range(plan.count)
        if n_in <= plan.start[i] and plan.start[i] + plan.rows <= n_in + n_block
    ]
    outer = [i for i in range(plan.count) if i not in inner]
    for i in inner:
        pack_rows_of(plan, me, i, d_block, plan.start[i] - n_in, keep, send)
    for i in outer:
        low = max(plan.start[i], n_in) // 8 * 8
        high = min(-(-(plan.start[i] + plan.rows) // 8) * 8, n_in + n_block)
        if low < high:
            table[low:high] = d_block[low - n_in : high - n_in]
    wide = []
    for i in range(images):
        part = jnp.concatenate([above[i], gz[i], below[i]], axis=0).astype(F32)
        wide.append(three_columns(part, cols))
    load.wait()
    db_in = jnp.zeros((1, channels), F32)
    for i in range(images):
        total = g_f[i] + sum(
            mm(wide[i][dy * cols : dy * cols + tokens], w1t[dy * kept : (dy + 1) * kept])
            for dy in range(3)
        )
        low = total.astype(BF)
        db_in = db_in + jnp.sum(low.astype(F32), axis=0, keepdims=True)
        if i == 0:
            late.wait()
        for dy in range(3):
            at = slice(dy * kept_in, (dy + 1) * kept_in)
            part = mm_tn(c3[i, (1 + dy) * cols : (1 + dy) * cols + tokens], low)
            table[at] = part if i == 0 else table[at] + part
    at = n_in + n_block
    table[at : at + 8] = jnp.concatenate(
        [db_in, d_rows[0:3], jnp.zeros((4, channels), F32)], axis=0
    )
    for i in outer:
        pack_rows_of(plan, me, i, table, plan.start[i], keep, send)


def snr_weights(timesteps):
    beta_sched = np.linspace(0.00085**0.5, 0.012**0.5, 1000, dtype=np.float64) ** 2
    alpha_bar = np.cumprod(1.0 - beta_sched)
    snr_value = alpha_bar / (1.0 - alpha_bar)
    lookup = jnp.asarray(np.minimum(snr_value, SNR_CAP) / snr_value, F32)
    hit_table = timesteps[:, None] == jnp.arange(1000, dtype=jnp.int32)[None, :]
    return jnp.sum(jnp.where(hit_table, lookup[None, :], 0.0), axis=1)


def shift_rows(value, step):
    count = lax.axis_size("sp")
    pairs = [(i, i + step) for i in range(count) if 0 <= i + step < count]
    return lax.ppermute(value, "sp", pairs)


def everywhere(payload):
    return lax.all_to_all(payload, ("sp", "hd"), 0, 0, tiled=True)


def body(
    cond, resid, context, noise, timesteps, step, query_weight, key_weight, value_weight,
    out_weight, pred_weight, master, first_moment, second_moment,
):
    images, row_count, cols, in_chan = cond.shape
    channels = resid.shape[-1]
    out_chan = noise.shape[-1]
    words = context.shape[2]
    tokens = row_count * cols
    all_tokens = images * tokens
    sp, hd = lax.axis_size("sp"), lax.axis_size("hd")
    plan = Plan(sp, hd, master.shape[0], channels)
    height = row_count * sp
    elements = images * hd * height * cols * channels
    heads = channels // HDIM
    n_in, n_one, n_two = 9 * in_chan, 9 * channels, channels
    at_sp = lax.axis_index("sp")
    place = jnp.stack(
        [
            at_sp * hd + lax.axis_index("hd"),
            (at_sp == 0).astype(jnp.int32),
            (at_sp == sp - 1).astype(jnp.int32),
        ]
    )
    snr = snr_weights(timesteps.reshape(-1))
    wide, kept, kept_in = tokens + 2 * cols, 3 * channels, 3 * in_chan

    def edges():
        low = shift_rows(cond[:, row_count - 2 :], 1).reshape(images, 2 * cols, in_chan)
        high = shift_rows(cond[:, :2], -1).reshape(images, 2 * cols, in_chan)
        return low, high

    def prepare(low, high):
        return call(
            functools.partial(prepare_kernel, cols),
            [
                ((images, wide + 2 * cols, kept_in), BF),
                ((images, channels, LANES), BF),
                ((images, channels, LANES), BF),
            ],
            [
                cond.reshape(images, tokens, in_chan), low, high,
                context.reshape(images, words, -1), key_weight.T, value_weight.T,
            ],
            free=(0, 3, 4, 5),
            flops=4 << 30,
        )

    gathered, (c3, k_t, v_t) = gather_parameters(plan, master, edges, prepare)
    line = ((plan.count, 1, LANES), F32)
    per_image = (images, tokens, channels)
    w1t, w_two, trailing, feature, relu_low, x3, payload = call(
        functools.partial(forward_kernel, plan, cols),
        [
            ((n_one, channels), BF),
            ((n_two, channels), BF),
            ((8, channels), F32),
            (per_image, F32),
            (per_image, BF),
            ((images, wide, kept), BF),
            line,
        ],
        [place, snr, *gathered, c3],
        scratch=[
            VMEM((plan.table, channels), F32),
            VMEM((n_in + n_one + n_two, channels), BF),
            VMEM((n_one, channels), BF),
            VMEM((images, wide + 2 * cols, kept_in), BF),
            VMEM(per_image, F32),
            VMEM(per_image, BF),
            VMEM((images, wide, kept), BF),
            DMA((2 + 4 * images,)),
        ],
        smem=(0, 1),
        far=(6,),
        far_out=(0, 1, 3, 4, 5),
        flops=4 << 30,
    )
    sums = everywhere(payload)
    g, u, payload = call(
        functools.partial(
            attention_kernel, plan, (elements, height * cols * out_chan, words)
        ),
        [(per_image, F32), ((8, channels), F32), line],
        [
            snr, sums, trailing, jnp.transpose(noise, (0, 1, 3, 2)), k_t, v_t, pred_weight.T,
            feature, resid.reshape(per_image), query_weight, out_weight,
        ],
        scratch=[
            VMEM(per_image, F32),
            VMEM(per_image, BF),
            VMEM((channels, channels), BF),
            VMEM((channels, channels), BF),
            VMEM(per_image, F32),
            VMEM((images, channels, heads * LANES), BF),
            VMEM((images, channels, heads * LANES), BF),
            DMA((2 + 3 * images,)),
        ],
        smem=(0,),
        far=(7, 8, 9, 10),
        far_out=(0,),
        flops=4 << 30,
    )
    sums_two = everywhere(payload)
    by_g, by_feature = call(
        back_kernel,
        [(per_image, F32), (per_image, F32)],
        [g, feature, relu_low, w_two],
        scratch=[
            VMEM(per_image, F32),
            VMEM(per_image, F32),
            VMEM(per_image, BF),
            VMEM((channels, channels), BF),
            DMA((4,)),
        ],
        far=(0, 1, 2, 3),
        flops=4 << 30,
    )
    scalars, gz, edge_top, edge_bottom = call(
        functools.partial(solve_kernel, cols, elements),
        [
            ((8, LANES), F32),
            (per_image, BF),
            ((images, cols, channels), BF),
            ((images, cols, channels), BF),
        ],
        [sums, sums_two, by_g, by_feature],
        flops=1 << 29,
    )
    above = shift_rows(edge_bottom, 1)
    below = shift_rows(edge_top, -1)
    d_block, d_rows, g_f = call(
        functools.partial(block_weight_kernel, cols),
        [((n_one + n_two, channels), F32), ((8, channels), F32), (per_image, F32)],
        [scalars, u, gz, x3, relu_low, g, feature],
        scratch=[
            VMEM((images, wide, kept), BF),
            VMEM(per_image, BF),
            VMEM(per_image, F32),
            VMEM(per_image, F32),
            DMA((images + 3,)),
        ],
        far=(3, 4, 5, 6),
        flops=2 << 30,
    )
    keep, send = call(
        functools.partial(input_kernel, plan, cols),
        [
            ((plan.half + 1, plan.packed, LANES), BF),
            ((plan.half + 1, plan.packed, LANES), BF),
        ],
        [place, gz, above, below, g_f, d_block, d_rows, w1t, c3],
        scratch=[
            VMEM((plan.table, channels), F32),
            VMEM((n_one, channels), BF),
            VMEM((images, wide + 2 * cols, kept_in), BF),
            DMA((2,)),
        ],
        smem=(0,),
        far=(7, 8),
        flops=4 << 30,
    )
    grad_share = scatter_gradient(plan, keep, send)
    steps_done = step[0].astype(F32)
    first_new = BETA_ONE * first_moment + (1.0 - BETA_ONE) * grad_share
    second_new = BETA_TWO * second_moment + (1.0 - BETA_TWO) * grad_share * grad_share
    first_hat = first_new / (1.0 - BETA_ONE**steps_done)
    second_hat = second_new / (1.0 - BETA_TWO**steps_done)
    new_master = master - RATE * (first_hat / (jnp.sqrt(second_hat) + EPS_ADAM) + DECAY * master)
    return (scalars[0, 0], new_master, first_new, second_new)


def solution(mesh):
    shard = P(("sp", "hd"))
    placed = (
        P("hd", "sp", None, None),
        P("hd", "sp", None, None),
        P("hd", None, None, None),
        P("hd", "sp", None, None),
        P("hd", None),
        P(),
        P(),
        P(),
        P(),
        P(),
        P(),
        shard,
        shard,
        shard,
    )
    return jax.shard_map(
        body,
        mesh=mesh,
        in_specs=placed,
        out_specs=(P(), shard, shard, shard),
        check_vma=False,
    )
```

```python
import functools

import jax
import jax.numpy as jnp
import numpy as np
from jax import lax
from jax.experimental import pallas as pl
from jax.experimental.pallas import tpu as pltpu
from jax.sharding import PartitionSpec as P

HDIM = 40
LANES = 128
EPS_NORM = 1e-05
RATE = 0.05
DECAY = 0.01
BETA_ONE = 0.5
BETA_TWO = 0.5
EPS_ADAM = 1e-08
SNR_CAP = 5.0
VMEM, HBM, DMA = pltpu.VMEM, pltpu.HBM, pltpu.SemaphoreType.DMA
BF = jnp.bfloat16
F32 = jnp.float32


def mm(a, b):
    return jnp.dot(a, b, preferred_element_type=F32)


def mm_nt(a, b):
    return lax.dot_general(a, b, (((1,), (1,)), ((), ())), preferred_element_type=F32)


def mm_tn(a, b):
    return lax.dot_general(a, b, (((0,), (0,)), ((), ())), preferred_element_type=F32)


def call(
    kernel, outs, ins, scratch=(), far=(), far_out=(), smem=(), free=(), far_like=(), flops=0,
    limit=40,
):
    def space(i):
        return pltpu.SMEM if i in smem else pl.ANY if i in far else VMEM

    def hold(i, x):
        return x if i in smem or i in free else pltpu.with_memory_space_constraint(x, HBM if i in far else VMEM)

    return pl.pallas_call(
        kernel,
        out_shape=[
            jax.ShapeDtypeStruct(*o) if i in far_like else (HBM if i in far_out else VMEM)(*o)
            for i, o in enumerate(outs)
        ],
        in_specs=[pl.BlockSpec(memory_space=space(i)) for i in range(len(ins))],
        out_specs=[
            pl.BlockSpec(memory_space=pl.ANY if i in far_out else VMEM) for i in range(len(outs))
        ],
        scratch_shapes=list(scratch),
        compiler_params=pltpu.CompilerParams(vmem_limit_bytes=limit * 1024 * 1024),
        cost_estimate=pl.CostEstimate(flops=flops, bytes_accessed=1 << 20, transcendentals=0),
    )(*[hold(i, x) for i, x in enumerate(ins)])


def start(source, target, sem):
    copy = pltpu.make_async_copy(source, target, sem)
    copy.start()
    return copy


class Plan:
    def __init__(self, sp, hd, length, channels):
        self.sp, self.hd, self.count = sp, hd, sp * hd
        self.length, self.channels = length, channels
        self.start = [length * i // channels for i in range(self.count)]
        need = max(
            -(-(length * i % channels + length) // channels) for i in range(self.count)
        )
        self.rows = -(-need // 32) * 32
        self.packed = self.rows * channels // LANES
        self.part_a = -(-self.packed // 32) * 16
        self.part_b = self.packed - self.part_a
        self.table = -(-(self.start[-1] + self.rows) // 8) * 8
        self.nz, self.nx = max(sp // 2, 1), min(sp, 2)
        self.ny, self.nk = max(hd // 2, 1), min(hd, 2)
        self.group_z = ("sp", sp, self.nx, self.nz)
        self.group_x = ("sp", sp, 1, self.nx)
        self.group_y = ("hd", hd, self.nk, self.ny)
        self.group_k = ("hd", hd, 1, self.nk)
        self.half = self.count // self.nk

    def place(self, owner, me):
        off = owner ^ me
        off_sp, off_hd = off // self.hd, off % self.hd
        z, x = off_sp // self.nx, off_sp % self.nx
        y, k = off_hd // self.nk, off_hd % self.nk
        return k, (y * self.nx + x) * self.nz + z, (x * self.ny + y) * self.nz + z


def swap(value, group, step):
    axis, count, stride, _ = group
    return lax.ppermute(value, axis, [(i, i ^ (step * stride)) for i in range(count)])


def spread(block, group):
    return jnp.concatenate([block] + [swap(block, group, e) for e in range(1, group[3])], axis=0)


def collect(total, group):
    size = total.shape[0] // group[3]
    out = total[:size]
    for e in range(1, group[3]):
        out = out + swap(total[e * size : (e + 1) * size].astype(BF), group, e).astype(F32)
    return out


def pack_rows(table):
    rows = table.shape[0]
    tail = table[:, 2 * LANES :]
    tail = jnp.concatenate([tail[: rows // 2], tail[rows // 2 :]], axis=1)
    return jnp.concatenate([table[:, :LANES], table[:, LANES : 2 * LANES], tail], axis=0)


def unpack_rows(packed, rows):
    tail = packed[2 * rows :]
    half = tail.shape[1] // 2
    tail = jnp.concatenate([tail[:, :half], tail[:, half:]], axis=0)
    return jnp.concatenate([packed[:rows], packed[rows : 2 * rows], tail], axis=1)


def gather_parameters(plan, master, edges, prepare):
    me = lax.axis_index("sp") * plan.hd + lax.axis_index("hd")
    shift = lax.rem(me * plan.length, plan.channels)
    total = plan.rows * plan.channels
    flat = jnp.pad(master, (plan.channels, total - plan.length))
    flat = lax.dynamic_slice(flat, (plan.channels - shift,), (total,))
    packed = pack_rows(flat.reshape(plan.rows, plan.channels).astype(BF))[None]
    packed = spread(packed, plan.group_z)
    packed, edges = lax.optimization_barrier((packed, edges()))
    part_a, part_b = packed[:, : plan.part_a], packed[:, plan.part_a :]
    part_a, part_b = spread(part_a, plan.group_x), spread(part_b, plan.group_y)
    part_a, part_b = spread(part_a, plan.group_y), spread(part_b, plan.group_x)
    part_a, part_b, ready = lax.optimization_barrier((part_a, part_b, prepare(*edges)))
    if plan.nk == 1:
        return (part_a, part_a, part_b, part_b), ready
    other_a, other_b = swap(part_a, plan.group_k, 1), swap(part_b, plan.group_k, 1)
    return (part_a, other_a, part_b, other_b), ready


def scatter_gradient(plan, keep, send):
    total = keep[: plan.half].astype(F32)
    if plan.nk > 1:
        total = total + swap(send, plan.group_k, 1)[: plan.half].astype(F32)
    part_a, part_b = total[:, : plan.part_a], total[:, plan.part_a :]
    for group_a, group_b in (
        (plan.group_y, plan.group_x),
        (plan.group_x, plan.group_y),
    ):
        part_a, part_b = collect(part_a, group_a), collect(part_b, group_b)
    packed = collect(jnp.concatenate([part_a, part_b], axis=1), plan.group_z)[0]
    flat = unpack_rows(packed, plan.rows).reshape(-1)
    me = lax.axis_index("sp") * plan.hd + lax.axis_index("hd")
    shift = lax.rem(me * plan.length, plan.channels)
    return lax.dynamic_slice(flat, (shift,), (plan.length,))


def three_columns(values, cols):
    tokens = values.shape[0]
    col = lax.broadcasted_iota(jnp.int32, values.shape, 0) % cols
    left = jnp.where(col == 0, 0.0, pltpu.roll(values, 1, 0))
    right = jnp.where(col == cols - 1, 0.0, pltpu.roll(values, tokens - 1, 0))
    return jnp.concatenate([left, values, right], axis=1).astype(BF)


def lane_pick(row, lane):
    ids = lax.broadcasted_iota(jnp.int32, row.shape, 1)
    return jnp.sum(jnp.where(ids == lane, row, 0.0))


def lane_row(pairs):
    ids = lax.broadcasted_iota(jnp.int32, (1, LANES), 1)
    row = jnp.zeros((1, LANES), F32)
    for lane, value in pairs:
        row = jnp.where(ids == lane, value, row)
    return row


def prepare_kernel(
    cols, heads, cond, low, high, context, wk_t, wv_t, resid, wq, wo,
    c3, keys, keys_t, values, values_t, resid_t, wq_t, wo_t,
):
    images = cond.shape[0]
    channels, words = wk_t.shape[0], context.shape[1]
    room = keys.shape[2]
    pad = jnp.zeros((channels, LANES - words), F32)
    for i in range(images):
        wide = jnp.concatenate([low[i], cond[i], high[i]], axis=0).astype(F32)
        c3[i] = three_columns(wide, cols)
        for weight, flat, tall in ((wk_t, keys, keys_t), (wv_t, values, values_t)):
            turned = jnp.concatenate([mm_nt(weight[...], context[i]), pad], axis=1)
            for h in range(heads):
                part = turned[h * HDIM : (h + 1) * HDIM]
                tall[i, h] = part[:, :room].astype(BF)
                part = jnp.concatenate([part, jnp.zeros((LANES - HDIM, LANES), F32)], axis=0)
                flat[i, h] = part.T[:room, :HDIM].astype(BF)
        resid_t[i] = resid[i].astype(F32).T.astype(BF)
    wq_t[...] = wq[...].astype(F32).T.astype(BF)
    wo_t[...] = wo[...].astype(F32).T.astype(BF)


def unpack_table(plan, me, own_a, other_a, own_b, other_b, table, owners):
    rows, split = plan.rows, plan.part_a
    for i in owners:
        k, at_a, at_b = plan.place(i, me)
        own = jnp.full((1, 1), k, jnp.int32) == 0
        a = jnp.where(own, own_a[at_a].astype(F32), other_a[at_a].astype(F32))
        b = jnp.where(own, own_b[at_b].astype(F32), other_b[at_b].astype(F32))
        begin = plan.start[i]
        old = table[begin : begin + 1, :] if i > 0 else None
        table[begin : begin + rows, :LANES] = a[:rows]
        table[begin : begin + rows, LANES : 2 * LANES] = jnp.concatenate(
            [a[rows:], b[: 2 * rows - split]], axis=0
        )
        tail = b[2 * rows - split :]
        table[begin : begin + rows // 2, 2 * LANES :] = tail[:, : LANES // 2]
        table[begin + rows // 2 : begin + rows, 2 * LANES :] = tail[:, LANES // 2 :]
        if i > 0:
            table[begin : begin + 1, :] += old


def forward_kernel(
    plan, cols, place, snr, own_a, other_a, own_b, other_b, c3_far,
    w1t_far, w_two_far, trailing, feature_far, relu_far, x3_far, payload,
    table, weights, w1t, c3, feature, relu_low, x3, sems,
):
    me, first, last = place[0], place[1], place[2]
    images, wide, kept_in = c3.shape
    load = [start(c3_far.at[i], c3.at[i], sems.at[i]) for i in range(images)]
    count, channels = weights.shape
    tokens = wide - 4 * cols
    more = tokens + 2 * cols
    kept = 3 * channels
    n_in = 3 * kept_in
    base_two = n_in + 3 * kept
    blocks = (own_a, other_a, own_b, other_b, table)
    early = [i for i in range(plan.count) if plan.start[i] < n_in]
    unpack_table(plan, me, *blocks, early)
    weights[:n_in] = table[:n_in].astype(BF)
    for copy in load:
        copy.wait()
    a_one = [
        sum(
            mm(c3[i, dy * cols : dy * cols + more], weights[dy * kept_in : (dy + 1) * kept_in])
            for dy in range(3)
        )
        for i in range(images)
    ]
    unpack_table(plan, me, *blocks, range(len(early), plan.count))
    weights[n_in:] = table[n_in:count].astype(BF)
    for row in range(9):
        at = n_in + (8 - row) * channels
        w1t[row * channels : (row + 1) * channels] = table[at : at + channels].T.astype(BF)
    first_store = start(w1t, w1t_far, sems.at[1 + 4 * images])
    stores = [first_store, start(weights.at[base_two : base_two + channels], w_two_far, sems.at[images])]
    trailing[...] = jnp.concatenate([table[count : count + 4], jnp.zeros((4, channels), F32)], axis=0)
    b_in, b_one, b_two = trailing[0:1], trailing[1:2], trailing[2:3]
    square = jnp.zeros((1, 1), F32)
    row = lax.broadcasted_iota(jnp.int32, (more, channels), 0) // cols
    outside = ((row == 0) & (first == 1)) | ((row == tokens // cols + 1) & (last == 1))
    for i in range(images):
        a_one[i] = a_one[i] + b_in
        a_low = jnp.where(outside, 0.0, a_one[i]).astype(BF).astype(F32)
        x3[i] = three_columns(a_low, cols)
        stores.append(start(x3.at[i], x3_far.at[i], sems.at[images + 1 + 3 * i]))
    for i in range(images):
        pre_relu = b_one + sum(
            mm(
                x3[i, dy * cols : dy * cols + tokens],
                weights[n_in + dy * kept : n_in + (dy + 1) * kept],
            )
            for dy in range(3)
        )
        relu = jnp.maximum(pre_relu, 0.0).astype(BF)
        relu_low[i] = relu
        stores.append(start(relu_low.at[i], relu_far.at[i], sems.at[images + 2 + 3 * i]))
        out = mm(relu, weights[base_two : base_two + channels]) + b_two
        out = out + a_one[i][cols : cols + tokens]
        feature[i] = out
        stores.append(start(feature.at[i], feature_far.at[i], sems.at[images + 3 + 3 * i]))
        square = square + jnp.sum(out * out)
    total = snr[0]
    for i in range(1, images):
        total = total + snr[i]
    line = lane_row([(0, square), (1, total)])
    payload[...] = jnp.broadcast_to(line[None], payload.shape)
    for copy in stores:
        copy.wait()


def norm_of(line, elements):
    return lax.rsqrt(jnp.full((1, 1), lane_pick(line, 0) / elements + EPS_NORM, F32))


def attention_kernel(
    plan, sizes, snr, sums, trailing, noise_t, wp_t,
    feature_far, resid_far, wqt_far, keys_far, valuest_far, wot_far, wo_far, values_far, keyst_far, wq_far,
    g_far, u_out, payload,
    feature, resid, wqt, keys, valuest, wot, wo, values, keyst, wq, g_out, sems,
):
    elements, loss_count, words = sizes
    images, tokens, channels = feature.shape
    heads, room = keys.shape[1:3]
    each = range(images)
    loads = [[], [], []]
    pairs = (
        (wqt_far, wqt, 0), (keys_far, keys, 0), (valuest_far, valuest, 1), (wot_far, wot, 1),
        (wo_far, wo, 2), (values_far, values, 2), (keyst_far, keyst, 2), (wq_far, wq, 2),
    )
    for i in each:
        loads[0].append(start(feature_far.at[i], feature.at[i], sems.at[2 * i]))
        loads[0].append(start(resid_far.at[i], resid.at[i], sems.at[2 * i + 1]))
    for j, (far, near, group) in enumerate(pairs):
        loads[group].append(start(far, near, sems.at[2 * images + j]))
    line = jnp.sum(sums[...], axis=0)
    scale = norm_of(line, elements)
    denom = lane_pick(line, 1) / plan.sp * loss_count
    inject = trailing[3:4]
    column = jnp.broadcast_to(inject, (LANES, channels)).T[:, 0:1] * scale
    root = HDIM ** (-0.5)
    out_chan, width = noise_t.shape[2:]
    spare = jnp.zeros((16 - out_chan, channels), F32)
    wide_pred = jnp.concatenate([wp_t[...].astype(F32), spare], axis=0).astype(BF)
    known = lax.broadcasted_iota(jnp.int32, (room, tokens), 0) < words
    for copy in loads[0]:
        copy.wait()
    injected, scores = [], []
    for i in each:
        injected.append(resid[i].astype(F32) + column * feature[i].T)
        query = mm(wqt[...], injected[i].astype(BF))
        parts = [query[h * HDIM : (h + 1) * HDIM].astype(BF) for h in range(heads)]
        scores.append([mm(keys[i, h], parts[h]) for h in range(heads)])
    attn = []
    for i in each:
        attn.append([])
        for h in range(heads):
            part = jnp.where(known, scores[i][h] * root, -1e30)
            part = jnp.exp(part - jnp.max(part, axis=0, keepdims=True))
            attn[i].append(part / jnp.sum(part, axis=0, keepdims=True))
    for copy in loads[1]:
        copy.wait()
    loss = jnp.zeros((1, 1), F32)
    g_y, g_attn = [], []
    for i in each:
        mixed = [mm(valuest[i, h], attn[i][h].astype(BF)) for h in range(heads)]
        after = injected[i] + mm(wot[...], jnp.concatenate(mixed, axis=0).astype(BF))
        pred = mm(wide_pred, after.astype(BF))
        noise = jnp.concatenate([noise_t[i, r] for r in range(tokens // width)], axis=1)
        noise = jnp.concatenate([noise, jnp.zeros((16 - out_chan, tokens), F32)], axis=0)
        error = pred - noise
        loss = loss + snr[i] * jnp.sum(error * error)
        g_pred = (2.0 * snr[i] / denom) * error
        g_y.append(mm_tn(wide_pred, g_pred.astype(BF)))
        if i == 0:
            for copy in loads[2]:
                copy.wait()
        g_mixed = mm(wo[...], g_y[i].astype(BF))
        parts = [g_mixed[h * HDIM : (h + 1) * HDIM].astype(BF) for h in range(heads)]
        g_attn.append([mm(values[i, h], parts[h]) for h in range(heads)])
    g_scores = []
    for i in each:
        g_scores.append([])
        for h in range(heads):
            inner = jnp.sum(attn[i][h] * g_attn[i][h], axis=0, keepdims=True)
            g_scores[i].append((attn[i][h] * (g_attn[i][h] - inner)).astype(BF))
    u = jnp.zeros((1, channels), F32)
    stores = []
    for i in each:
        parts = [mm(keyst[i, h], g_scores[i][h]) * root for h in range(heads)]
        g_x = g_y[i] + mm(wq[...], jnp.concatenate(parts, axis=0).astype(BF))
        g_x = g_x.T
        g_out[i] = scale * (inject * g_x)
        stores.append(start(g_out.at[i], g_far.at[i], sems.at[2 * images + len(pairs) + i]))
        u = u + jnp.sum(g_x * feature[i], axis=0, keepdims=True)
    u_out[...] = jnp.broadcast_to(u, u_out.shape)
    cross = jnp.sum(inject * u)
    payload[...] = jnp.broadcast_to(lane_row([(0, loss / denom), (1, cross)])[None], payload.shape)
    for copy in stores:
        copy.wait()


def back_kernel(
    g_far, feature_far, relu_far, w_two_far, x3_far, by_g, by_feature, x3,
    g, feature, relu, w_two, sems,
):
    images, tokens, channels = by_g.shape
    loads = [start(w_two_far, w_two, sems.at[0])]
    pairs = ((feature_far, feature), (relu_far, relu), (g_far, g), (x3_far, x3))
    for j, (far, near) in enumerate(pairs):
        loads.append(start(far, near, sems.at[1 + j]))
    for copy in loads[:3]:
        copy.wait()
    for i in range(images):
        back = mm_nt(feature[i].astype(BF), w_two[...])
        by_feature[i] = jnp.where(relu[i].astype(F32) > 0, back, 0.0)
    loads[3].wait()
    for i in range(images):
        back = mm_nt(g[i].astype(BF), w_two[...])
        by_g[i] = jnp.where(relu[i].astype(F32) > 0, back, 0.0)
    loads[4].wait()


def solve_kernel(
    cols, elements, sums, sums_two, by_g, by_feature, scalars, gz, edge_top, edge_bottom
):
    images, tokens, channels = gz.shape
    scale = norm_of(jnp.sum(sums[...], axis=0), elements)
    line = jnp.sum(sums_two[...], axis=0)
    pull = scale * scale * scale * (lane_pick(line, 1) / elements)
    pairs = [(0, jnp.full((1, 1), lane_pick(line, 0), F32)), (1, pull), (2, scale)]
    scalars[...] = jnp.broadcast_to(lane_row(pairs), scalars.shape)
    for i in range(images):
        back = (by_g[i] - pull * by_feature[i]).astype(BF)
        gz[i] = back
        edge_top[i] = back[:cols]
        edge_bottom[i] = back[tokens - cols :]


def block_weight_kernel(
    cols, scalars, u, gz, x3, relu_far, g_far, feature_far,
    d_block, d_rows, g_f, relu, g, feature, sems,
):
    images, tokens, channels = gz.shape
    kept = 3 * channels
    late = [
        start(far, near, sems.at[j])
        for j, (far, near) in enumerate(((relu_far, relu), (g_far, g), (feature_far, feature)))
    ]
    pull, scale = scalars[0:1, 1:2], scalars[0:1, 2:3]
    rows = [jnp.zeros((1, channels), F32), jnp.zeros((1, channels), F32)]
    for i in range(images):
        for dy in range(3):
            at = slice(dy * kept, (dy + 1) * kept)
            part = mm_tn(x3[i, dy * cols : dy * cols + tokens], gz[i])
            d_block[at] = part if i == 0 else d_block[at] + part
        rows[0] = rows[0] + jnp.sum(gz[i].astype(F32), axis=0, keepdims=True)
    for copy in late:
        copy.wait()
    at = slice(3 * kept, 3 * kept + channels)
    for i in range(images):
        g_f[i] = g[i] - pull * feature[i]
        low = g_f[i].astype(BF)
        part = mm_tn(relu[i], low)
        d_block[at] = part if i == 0 else d_block[at] + part
        rows[1] = rows[1] + jnp.sum(low.astype(F32), axis=0, keepdims=True)
    d_rows[...] = jnp.concatenate(rows + [scale * u[0:1], jnp.zeros((5, channels), F32)], axis=0)


def pack_rows_of(plan, me, i, table, begin, keep, send):
    rows, split = plan.rows, plan.part_a
    k, at_a, at_b = plan.place(i, me)
    half = begin + rows // 2
    one = table[begin : begin + rows, :LANES]
    two = table[begin : begin + rows, LANES : 2 * LANES]
    tail = jnp.concatenate(
        [table[begin:half, 2 * LANES :], table[half : begin + rows, 2 * LANES :]], axis=1
    )
    a = jnp.concatenate([one, two[: split - rows]], axis=0).astype(BF)
    b = jnp.concatenate([two[split - rows :], tail], axis=0).astype(BF)
    for wanted, out in ((0, keep), (1, send)):
        hit = k == wanted
        out[jnp.where(hit, at_a, plan.half), :split] = a
        out[jnp.where(hit, at_b, plan.half), split:] = b


def input_kernel(
    plan, cols, place, gz, above, below, g_f, d_block, d_rows, w1t_far, c3_far,
    keep, send, table, w1t, c3, sems,
):
    me = place[0]
    images, tokens, channels = gz.shape
    kept, kept_in = 3 * channels, c3.shape[2]
    load = start(w1t_far, w1t, sems.at[0])
    late = start(c3_far, c3, sems.at[1])
    n_in, n_block = 3 * kept_in, d_block.shape[0]
    inner = [
        i for i in range(plan.count)
        if n_in <= plan.start[i] and plan.start[i] + plan.rows <= n_in + n_block
    ]
    outer = [i for i in range(plan.count) if i not in inner]
    for i in inner:
        pack_rows_of(plan, me, i, d_block, plan.start[i] - n_in, keep, send)
    for i in outer:
        low = max(plan.start[i], n_in) // 8 * 8
        high = min(-(-(plan.start[i] + plan.rows) // 8) * 8, n_in + n_block)
        if low < high:
            table[low:high] = d_block[low - n_in : high - n_in]
    wide = []
    for i in range(images):
        part = jnp.concatenate([above[i], gz[i], below[i]], axis=0).astype(F32)
        wide.append(three_columns(part, cols))
    load.wait()
    db_in = jnp.zeros((1, channels), F32)
    for i in range(images):
        total = g_f[i] + sum(
            mm(wide[i][dy * cols : dy * cols + tokens], w1t[dy * kept : (dy + 1) * kept])
            for dy in range(3)
        )
        low = total.astype(BF)
        db_in = db_in + jnp.sum(low.astype(F32), axis=0, keepdims=True)
        if i == 0:
            late.wait()
        for dy in range(3):
            at = slice(dy * kept_in, (dy + 1) * kept_in)
            part = mm_tn(c3[i, (1 + dy) * cols : (1 + dy) * cols + tokens], low)
            table[at] = part if i == 0 else table[at] + part
    at = n_in + n_block
    table[at : at + 8] = jnp.concatenate(
        [db_in, d_rows[0:3], jnp.zeros((4, channels), F32)], axis=0
    )
    for i in outer:
        pack_rows_of(plan, me, i, table, plan.start[i], keep, send)


def snr_weights(timesteps):
    beta_sched = np.linspace(0.00085**0.5, 0.012**0.5, 1000, dtype=np.float64) ** 2
    alpha_bar = np.cumprod(1.0 - beta_sched)
    snr_value = alpha_bar / (1.0 - alpha_bar)
    lookup = jnp.asarray(np.minimum(snr_value, SNR_CAP) / snr_value, F32)
    hit_table = timesteps[:, None] == jnp.arange(1000, dtype=jnp.int32)[None, :]
    return jnp.sum(jnp.where(hit_table, lookup[None, :], 0.0), axis=1)


def shift_rows(value, step):
    count = lax.axis_size("sp")
    pairs = [(i, i + step) for i in range(count) if 0 <= i + step < count]
    return lax.ppermute(value, "sp", pairs)


def everywhere(payload):
    return lax.all_to_all(payload, ("sp", "hd"), 0, 0, tiled=True)


def body(
    cond, resid, context, noise, timesteps, step, query_weight, key_weight, value_weight,
    out_weight, pred_weight, master, first_moment, second_moment,
):
    images, row_count, cols, in_chan = cond.shape
    channels = resid.shape[-1]
    out_chan = noise.shape[-1]
    words = context.shape[2]
    tokens = row_count * cols
    all_tokens = images * tokens
    sp, hd = lax.axis_size("sp"), lax.axis_size("hd")
    plan = Plan(sp, hd, master.shape[0], channels)
    height = row_count * sp
    elements = images * hd * height * cols * channels
    heads = channels // HDIM
    n_in, n_one, n_two = 9 * in_chan, 9 * channels, channels
    at_sp = lax.axis_index("sp")
    place = jnp.stack(
        [
            at_sp * hd + lax.axis_index("hd"),
            (at_sp == 0).astype(jnp.int32),
            (at_sp == sp - 1).astype(jnp.int32),
        ]
    )
    snr = snr_weights(timesteps.reshape(-1))
    wide, kept, kept_in = tokens + 2 * cols, 3 * channels, 3 * in_chan

    def edges():
        low = shift_rows(cond[:, row_count - 2 :], 1).reshape(images, 2 * cols, in_chan)
        high = shift_rows(cond[:, :2], -1).reshape(images, 2 * cols, in_chan)
        return low, high

    def prepare(low, high):
        return call(
            functools.partial(prepare_kernel, cols, heads),
            [
                ((images, wide + 2 * cols, kept_in), BF),
                ((images, heads, room, HDIM), BF),
                ((images, heads, HDIM, room), BF),
                ((images, heads, room, HDIM), BF),
                ((images, heads, HDIM, room), BF),
                ((images, channels, tokens), BF),
                ((channels, channels), BF),
                ((channels, channels), BF),
            ],
            [
                cond.reshape(images, tokens, in_chan), low, high,
                context.reshape(images, words, -1), key_weight.T, value_weight.T,
                resid.reshape(images, tokens, channels), query_weight, out_weight,
            ],
            free=(0, 3, 4, 5, 6, 7, 8),
            far_like=(0, 1, 2, 3, 4, 5, 6, 7),
            flops=4 << 30,
        )

    room = -(-words // 16) * 16
    gathered, prepared = gather_parameters(plan, master, edges, prepare)
    c3, keys, keys_t, values, values_t, resid_t, wq_t, wo_t = prepared
    line = ((plan.count, 1, LANES), F32)
    per_image = (images, tokens, channels)
    w1t, w_two, trailing, feature, relu_low, x3, payload = call(
        functools.partial(forward_kernel, plan, cols),
        [
            ((n_one, channels), BF),
            ((n_two, channels), BF),
            ((8, channels), F32),
            (per_image, F32),
            (per_image, BF),
            ((images, wide, kept), BF),
            line,
        ],
        [place, snr, *gathered, c3],
        scratch=[
            VMEM((plan.table, channels), F32),
            VMEM((n_in + n_one + n_two, channels), BF),
            VMEM((n_one, channels), BF),
            VMEM((images, wide + 2 * cols, kept_in), BF),
            VMEM(per_image, F32),
            VMEM(per_image, BF),
            VMEM((images, wide, kept), BF),
            DMA((2 + 4 * images,)),
        ],
        smem=(0, 1),
        far=(6,),
        far_out=(0, 1, 3, 4, 5),
        flops=4 << 30,
    )
    sums = everywhere(payload)
    square = (channels, channels)
    g, u, payload = call(
        functools.partial(
            attention_kernel, plan, (elements, height * cols * out_chan, words)
        ),
        [(per_image, F32), ((8, channels), F32), line],
        [
            snr, sums, trailing, jnp.transpose(noise, (0, 1, 3, 2)), pred_weight.T,
            feature, resid_t, wq_t, keys, values_t, wo_t, out_weight, values, keys_t, query_weight,
        ],
        scratch=[
            VMEM(per_image, F32),
            VMEM((images, channels, tokens), BF),
            VMEM(square, BF),
            VMEM((images, heads, room, HDIM), BF),
            VMEM((images, heads, HDIM, room), BF),
            VMEM(square, BF),
            VMEM(square, BF),
            VMEM((images, heads, room, HDIM), BF),
            VMEM((images, heads, HDIM, room), BF),
            VMEM(square, BF),
            VMEM(per_image, F32),
            DMA((3 * images + 8,)),
        ],
        smem=(0,),
        far=tuple(range(5, 15)),
        far_out=(0,),
        flops=4 << 30,
    )
    sums_two = everywhere(payload)
    by_g, by_feature, x3 = call(
        back_kernel,
        [(per_image, F32), (per_image, F32), ((images, wide, kept), BF)],
        [g, feature, relu_low, w_two, x3],
        scratch=[
            VMEM(per_image, F32),
            VMEM(per_image, F32),
            VMEM(per_image, BF),
            VMEM((channels, channels), BF),
            DMA((5,)),
        ],
        far=(0, 1, 2, 3, 4),
        flops=4 << 30,
    )
    scalars, gz, edge_top, edge_bottom = call(
        functools.partial(solve_kernel, cols, elements),
        [
            ((8, LANES), F32),
            (per_image, BF),
            ((images, cols, channels), BF),
            ((images, cols, channels), BF),
        ],
        [sums, sums_two, by_g, by_feature],
        flops=1 << 29,
    )
    above = shift_rows(edge_bottom, 1)
    below = shift_rows(edge_top, -1)
    d_block, d_rows, g_f = call(
        functools.partial(block_weight_kernel, cols),
        [((n_one + n_two, channels), F32), ((8, channels), F32), (per_image, F32)],
        [scalars, u, gz, x3, relu_low, g, feature],
        scratch=[
            VMEM(per_image, BF),
            VMEM(per_image, F32),
            VMEM(per_image, F32),
            DMA((3,)),
        ],
        far=(4, 5, 6),
        flops=2 << 30,
    )
    keep, send = call(
        functools.partial(input_kernel, plan, cols),
        [
            ((plan.half + 1, plan.packed, LANES), BF),
            ((plan.half + 1, plan.packed, LANES), BF),
        ],
        [place, gz, above, below, g_f, d_block, d_rows, w1t, c3],
        scratch=[
            VMEM((plan.table, channels), F32),
            VMEM((n_one, channels), BF),
            VMEM((images, wide + 2 * cols, kept_in), BF),
            DMA((2,)),
        ],
        smem=(0,),
        far=(7, 8),
        flops=4 << 30,
    )
    grad_share = scatter_gradient(plan, keep, send)
    steps_done = step[0].astype(F32)
    first_new = BETA_ONE * first_moment + (1.0 - BETA_ONE) * grad_share
    second_new = BETA_TWO * second_moment + (1.0 - BETA_TWO) * grad_share * grad_share
    first_hat = first_new / (1.0 - BETA_ONE**steps_done)
    second_hat = second_new / (1.0 - BETA_TWO**steps_done)
    new_master = master - RATE * (first_hat / (jnp.sqrt(second_hat) + EPS_ADAM) + DECAY * master)
    return (scalars[0, 0], new_master, first_new, second_new)


def solution(mesh):
    shard = P(("sp", "hd"))
    placed = (
        P("hd", "sp", None, None),
        P("hd", "sp", None, None),
        P("hd", None, None, None),
        P("hd", "sp", None, None),
        P("hd", None),
        P(),
        P(),
        P(),
        P(),
        P(),
        P(),
        shard,
        shard,
        shard,
    )
    return jax.shard_map(
        body,
        mesh=mesh,
        in_specs=placed,
        out_specs=(P(), shard, shard, shard),
        check_vma=False,
    )
```

```python
import functools

import jax
import jax.numpy as jnp
import numpy as np
from jax import lax
from jax.experimental import pallas as pl
from jax.experimental.pallas import tpu as pltpu
from jax.sharding import PartitionSpec as P

HDIM = 40
LANES = 128
EPS_NORM = 1e-05
RATE = 0.05
DECAY = 0.01
BETA_ONE = 0.5
BETA_TWO = 0.5
EPS_ADAM = 1e-08
SNR_CAP = 5.0
VMEM, HBM, DMA = pltpu.VMEM, pltpu.HBM, pltpu.SemaphoreType.DMA
BF = jnp.bfloat16
F32 = jnp.float32


def mm(a, b):
    return jnp.dot(a, b, preferred_element_type=F32)


def mm_nt(a, b):
    return lax.dot_general(a, b, (((1,), (1,)), ((), ())), preferred_element_type=F32)


def mm_tn(a, b):
    return lax.dot_general(a, b, (((0,), (0,)), ((), ())), preferred_element_type=F32)


def call(
    kernel, outs, ins, scratch=(), far=(), far_out=(), smem=(), free=(), far_like=(), flops=0,
    limit=40,
):
    def space(i):
        return pltpu.SMEM if i in smem else pl.ANY if i in far else VMEM

    def hold(i, x):
        return x if i in smem or i in free else pltpu.with_memory_space_constraint(x, HBM if i in far else VMEM)

    return pl.pallas_call(
        kernel,
        out_shape=[
            jax.ShapeDtypeStruct(*o) if i in far_like else (HBM if i in far_out else VMEM)(*o)
            for i, o in enumerate(outs)
        ],
        in_specs=[pl.BlockSpec(memory_space=space(i)) for i in range(len(ins))],
        out_specs=[
            pl.BlockSpec(memory_space=pl.ANY if i in far_out else VMEM) for i in range(len(outs))
        ],
        scratch_shapes=list(scratch),
        compiler_params=pltpu.CompilerParams(vmem_limit_bytes=limit * 1024 * 1024),
        cost_estimate=pl.CostEstimate(flops=flops, bytes_accessed=1 << 20, transcendentals=0),
    )(*[hold(i, x) for i, x in enumerate(ins)])


def start(source, target, sem):
    copy = pltpu.make_async_copy(source, target, sem)
    copy.start()
    return copy


class Plan:
    def __init__(self, sp, hd, length, channels):
        self.sp, self.hd, self.count = sp, hd, sp * hd
        self.length, self.channels = length, channels
        self.start = [length * i // channels for i in range(self.count)]
        need = max(
            -(-(length * i % channels + length) // channels) for i in range(self.count)
        )
        self.rows = -(-need // 32) * 32
        self.packed = self.rows * channels // LANES
        self.part_a = -(-self.packed // 32) * 16
        self.part_b = self.packed - self.part_a
        self.table = -(-(self.start[-1] + self.rows) // 8) * 8
        self.nz, self.nx = max(sp // 2, 1), min(sp, 2)
        self.ny, self.nk = max(hd // 2, 1), min(hd, 2)
        self.group_z = ("sp", sp, self.nx, self.nz)
        self.group_x = ("sp", sp, 1, self.nx)
        self.group_y = ("hd", hd, self.nk, self.ny)
        self.group_k = ("hd", hd, 1, self.nk)
        self.half = self.count // self.nk

    def place(self, owner, me):
        off = owner ^ me
        off_sp, off_hd = off // self.hd, off % self.hd
        z, x = off_sp // self.nx, off_sp % self.nx
        y, k = off_hd // self.nk, off_hd % self.nk
        return k, (y * self.nx + x) * self.nz + z, (x * self.ny + y) * self.nz + z


def swap(value, group, step):
    axis, count, stride, _ = group
    return lax.ppermute(value, axis, [(i, i ^ (step * stride)) for i in range(count)])


def spread(block, group):
    return jnp.concatenate([block] + [swap(block, group, e) for e in range(1, group[3])], axis=0)


def collect(total, group):
    size = total.shape[0] // group[3]
    out = total[:size]
    for e in range(1, group[3]):
        out = out + swap(total[e * size : (e + 1) * size].astype(BF), group, e).astype(F32)
    return out


def pack_rows(table):
    rows = table.shape[0]
    tail = table[:, 2 * LANES :]
    tail = jnp.concatenate([tail[: rows // 2], tail[rows // 2 :]], axis=1)
    return jnp.concatenate([table[:, :LANES], table[:, LANES : 2 * LANES], tail], axis=0)


def unpack_rows(packed, rows):
    tail = packed[2 * rows :]
    half = tail.shape[1] // 2
    tail = jnp.concatenate([tail[:, :half], tail[:, half:]], axis=0)
    return jnp.concatenate([packed[:rows], packed[rows : 2 * rows], tail], axis=1)


def gather_parameters(plan, master, edges, prepare):
    me = lax.axis_index("sp") * plan.hd + lax.axis_index("hd")
    shift = lax.rem(me * plan.length, plan.channels)
    total = plan.rows * plan.channels
    flat = jnp.pad(master, (plan.channels, total - plan.length))
    flat = lax.dynamic_slice(flat, (plan.channels - shift,), (total,))
    packed = pack_rows(flat.reshape(plan.rows, plan.channels).astype(BF))[None]
    packed = spread(packed, plan.group_z)
    part_a, part_b = packed[:, : plan.part_a], packed[:, plan.part_a :]
    part_a, edges = lax.optimization_barrier((part_a, edges()))
    part_a, part_b = spread(part_a, plan.group_x), spread(part_b, plan.group_y)
    part_a, part_b = spread(part_a, plan.group_y), spread(part_b, plan.group_x)
    part_a, part_b, ready = lax.optimization_barrier((part_a, part_b, prepare(*edges)))
    if plan.nk == 1:
        return (part_a, part_a, part_b, part_b), ready
    other_a, other_b = swap(part_a, plan.group_k, 1), swap(part_b, plan.group_k, 1)
    return (part_a, other_a, part_b, other_b), ready


def scatter_gradient(plan, keep, send):
    total = keep[: plan.half].astype(F32)
    if plan.nk > 1:
        total = total + swap(send, plan.group_k, 1)[: plan.half].astype(F32)
    part_a, part_b = total[:, : plan.part_a], total[:, plan.part_a :]
    for group_a, group_b in (
        (plan.group_y, plan.group_x),
        (plan.group_x, plan.group_y),
    ):
        part_a, part_b = collect(part_a, group_a), collect(part_b, group_b)
    packed = collect(jnp.concatenate([part_a, part_b], axis=1), plan.group_z)[0]
    flat = unpack_rows(packed, plan.rows).reshape(-1)
    me = lax.axis_index("sp") * plan.hd + lax.axis_index("hd")
    shift = lax.rem(me * plan.length, plan.channels)
    return lax.dynamic_slice(flat, (shift,), (plan.length,))


def three_columns(values, cols):
    tokens = values.shape[0]
    col = lax.broadcasted_iota(jnp.int32, values.shape, 0) % cols
    left = jnp.where(col == 0, 0.0, pltpu.roll(values, 1, 0))
    right = jnp.where(col == cols - 1, 0.0, pltpu.roll(values, tokens - 1, 0))
    return jnp.concatenate([left, values, right], axis=1).astype(BF)


def neighbours(place, first, second):
    even = jnp.full((1, 1), place[3], jnp.int32) == 0
    return jnp.where(even, second, first), jnp.where(even, first, second)


def lane_pick(row, lane):
    ids = lax.broadcasted_iota(jnp.int32, row.shape, 1)
    return jnp.sum(jnp.where(ids == lane, row, 0.0))


def lane_row(pairs):
    ids = lax.broadcasted_iota(jnp.int32, (1, LANES), 1)
    row = jnp.zeros((1, LANES), F32)
    for lane, value in pairs:
        row = jnp.where(ids == lane, value, row)
    return row


def prepare_kernel(
    cols, heads, place, cond, first, second, context, wk_t, wv_t, resid, wq, wo,
    c3, keys, keys_t, values, values_t, resid_t, wq_t, wo_t,
):
    images = cond.shape[0]
    channels, words = wk_t.shape[0], context.shape[1]
    room = keys.shape[2]
    pad = jnp.zeros((channels, LANES - words), F32)
    for i in range(images):
        low, high = neighbours(place, first[i].astype(F32), second[i].astype(F32))
        wide = jnp.concatenate([low, cond[i].astype(F32), high], axis=0)
        c3[i] = three_columns(wide, cols)
        for weight, flat, tall in ((wk_t, keys, keys_t), (wv_t, values, values_t)):
            turned = jnp.concatenate([mm_nt(weight[...], context[i]), pad], axis=1)
            for h in range(heads):
                part = turned[h * HDIM : (h + 1) * HDIM]
                tall[i, h] = part[:, :room].astype(BF)
                part = jnp.concatenate([part, jnp.zeros((LANES - HDIM, LANES), F32)], axis=0)
                flat[i, h] = part.T[:room, :HDIM].astype(BF)
        resid_t[i] = resid[i].astype(F32).T.astype(BF)
    wq_t[...] = wq[...].astype(F32).T.astype(BF)
    wo_t[...] = wo[...].astype(F32).T.astype(BF)


def unpack_table(plan, me, own_a, other_a, own_b, other_b, table, owners):
    rows, split = plan.rows, plan.part_a
    for i in owners:
        k, at_a, at_b = plan.place(i, me)
        own = jnp.full((1, 1), k, jnp.int32) == 0
        a = jnp.where(own, own_a[at_a].astype(F32), other_a[at_a].astype(F32))
        b = jnp.where(own, own_b[at_b].astype(F32), other_b[at_b].astype(F32))
        begin = plan.start[i]
        old = table[begin : begin + 1, :] if i > 0 else None
        table[begin : begin + rows, :LANES] = a[:rows]
        table[begin : begin + rows, LANES : 2 * LANES] = jnp.concatenate(
            [a[rows:], b[: 2 * rows - split]], axis=0
        )
        tail = b[2 * rows - split :]
        table[begin : begin + rows // 2, 2 * LANES :] = tail[:, : LANES // 2]
        table[begin + rows // 2 : begin + rows, 2 * LANES :] = tail[:, LANES // 2 :]
        if i > 0:
            table[begin : begin + 1, :] += old


def forward_kernel(
    plan, cols, place, snr, own_a, other_a, own_b, other_b, c3_far,
    w1t_far, w_two_far, trailing, feature_far, relu_far, x3_far, payload,
    table, weights, w1t, c3, feature, relu_low, x3, sems,
):
    me, first, last = place[0], place[1], place[2]
    images, wide, kept_in = c3.shape
    load = [start(c3_far.at[i], c3.at[i], sems.at[i]) for i in range(images)]
    count, channels = weights.shape
    tokens = wide - 4 * cols
    more = tokens + 2 * cols
    kept = 3 * channels
    n_in = 3 * kept_in
    base_two = n_in + 3 * kept
    blocks = (own_a, other_a, own_b, other_b, table)
    early = [i for i in range(plan.count) if plan.start[i] < n_in]
    unpack_table(plan, me, *blocks, early)
    weights[:n_in] = table[:n_in].astype(BF)
    for copy in load:
        copy.wait()
    a_one = [
        mm(
            jnp.concatenate([c3[i, dy * cols : dy * cols + more] for dy in range(3)], axis=1),
            weights[:n_in],
        )
        for i in range(images)
    ]
    unpack_table(plan, me, *blocks, range(len(early), plan.count))
    weights[n_in:] = table[n_in:count].astype(BF)
    for row in range(9):
        at = n_in + (8 - row) * channels
        w1t[row * channels : (row + 1) * channels] = table[at : at + channels].T.astype(BF)
    first_store = start(w1t, w1t_far, sems.at[1 + 4 * images])
    stores = [first_store, start(weights.at[base_two : base_two + channels], w_two_far, sems.at[images])]
    trailing[...] = jnp.concatenate([table[count : count + 4], jnp.zeros((4, channels), F32)], axis=0)
    b_in, b_one, b_two = trailing[0:1], trailing[1:2], trailing[2:3]
    square = jnp.zeros((1, 1), F32)
    row = lax.broadcasted_iota(jnp.int32, (more, channels), 0) // cols
    outside = ((row == 0) & (first == 1)) | ((row == tokens // cols + 1) & (last == 1))
    for i in range(images):
        a_one[i] = a_one[i] + b_in
        a_low = jnp.where(outside, 0.0, a_one[i]).astype(BF).astype(F32)
        x3[i] = three_columns(a_low, cols)
        stores.append(start(x3.at[i], x3_far.at[i], sems.at[images + 1 + 3 * i]))
    for i in range(images):
        pre_relu = b_one + sum(
            mm(
                x3[i, dy * cols : dy * cols + tokens],
                weights[n_in + dy * kept : n_in + (dy + 1) * kept],
            )
            for dy in range(3)
        )
        relu = jnp.maximum(pre_relu, 0.0).astype(BF)
        relu_low[i] = relu
        stores.append(start(relu_low.at[i], relu_far.at[i], sems.at[images + 2 + 3 * i]))
        out = mm(relu, weights[base_two : base_two + channels]) + b_two
        out = out + a_one[i][cols : cols + tokens]
        feature[i] = out
        stores.append(start(feature.at[i], feature_far.at[i], sems.at[images + 3 + 3 * i]))
        square = square + jnp.sum(out * out)
    total = snr[0]
    for i in range(1, images):
        total = total + snr[i]
    line = lane_row([(0, square), (1, total)])
    payload[...] = jnp.broadcast_to(line[None], payload.shape)
    for copy in stores:
        copy.wait()


def norm_of(line, elements):
    return lax.rsqrt(jnp.full((1, 1), lane_pick(line, 0) / elements + EPS_NORM, F32))


def attention_kernel(
    plan, sizes, snr, sums, trailing, noise_t, wp_t,
    feature_far, resid_far, wqt_far, keys_far, valuest_far, wot_far, wo_far, values_far, keyst_far, wq_far,
    g_far, u_out, payload,
    feature, resid, wqt, keys, valuest, wot, wo, values, keyst, wq, g_out, sems,
):
    elements, loss_count, words = sizes
    images, tokens, channels = feature.shape
    heads, room = keys.shape[1:3]
    each = range(images)
    loads = [[], [], []]
    pairs = (
        (wqt_far, wqt, 0), (keys_far, keys, 0), (valuest_far, valuest, 1), (wot_far, wot, 1),
        (wo_far, wo, 2), (values_far, values, 2), (keyst_far, keyst, 2), (wq_far, wq, 2),
    )
    for i in each:
        loads[0].append(start(feature_far.at[i], feature.at[i], sems.at[2 * i]))
        loads[0].append(start(resid_far.at[i], resid.at[i], sems.at[2 * i + 1]))
    for j, (far, near, group) in enumerate(pairs):
        loads[group].append(start(far, near, sems.at[2 * images + j]))
    line = jnp.sum(sums[...], axis=0)
    scale = norm_of(line, elements)
    denom = lane_pick(line, 1) / plan.sp * loss_count
    inject = trailing[3:4]
    column = jnp.broadcast_to(inject, (LANES, channels)).T[:, 0:1] * scale
    root = HDIM ** (-0.5)
    out_chan, width = noise_t.shape[2:]
    spare = jnp.zeros((16 - out_chan, channels), F32)
    wide_pred = jnp.concatenate([wp_t[...].astype(F32), spare], axis=0).astype(BF)
    known = lax.broadcasted_iota(jnp.int32, (room, tokens), 0) < words
    for copy in loads[0]:
        copy.wait()
    injected, scores = [], []
    for i in each:
        injected.append(resid[i].astype(F32) + column * feature[i].T)
        query = mm(wqt[...], injected[i].astype(BF))
        parts = [query[h * HDIM : (h + 1) * HDIM].astype(BF) for h in range(heads)]
        scores.append([mm(keys[i, h], parts[h]) for h in range(heads)])
    attn = []
    for i in each:
        attn.append([])
        for h in range(heads):
            part = jnp.where(known, scores[i][h] * root, -1e30)
            part = jnp.exp(part - jnp.max(part, axis=0, keepdims=True))
            attn[i].append(part / jnp.sum(part, axis=0, keepdims=True))
    for copy in loads[1]:
        copy.wait()
    loss = jnp.zeros((1, 1), F32)
    g_y, g_attn = [], []
    for i in each:
        mixed = [mm(valuest[i, h], attn[i][h].astype(BF)) for h in range(heads)]
        after = injected[i] + mm(wot[...], jnp.concatenate(mixed, axis=0).astype(BF))
        pred = mm(wide_pred, after.astype(BF))
        noise = jnp.concatenate([noise_t[i, r] for r in range(tokens // width)], axis=1)
        noise = jnp.concatenate([noise, jnp.zeros((16 - out_chan, tokens), F32)], axis=0)
        error = pred - noise
        loss = loss + snr[i] * jnp.sum(error * error)
        g_pred = (2.0 * snr[i] / denom) * error
        g_y.append(mm_tn(wide_pred, g_pred.astype(BF)))
        if i == 0:
            for copy in loads[2]:
                copy.wait()
        g_mixed = mm(wo[...], g_y[i].astype(BF))
        parts = [g_mixed[h * HDIM : (h + 1) * HDIM].astype(BF) for h in range(heads)]
        g_attn.append([mm(values[i, h], parts[h]) for h in range(heads)])
    g_scores = []
    for i in each:
        g_scores.append([])
        for h in range(heads):
            inner = jnp.sum(attn[i][h] * g_attn[i][h], axis=0, keepdims=True)
            g_scores[i].append((attn[i][h] * (g_attn[i][h] - inner)).astype(BF))
    u = jnp.zeros((1, channels), F32)
    stores = []
    for i in each:
        parts = [mm(keyst[i, h], g_scores[i][h]) * root for h in range(heads)]
        g_x = g_y[i] + mm(wq[...], jnp.concatenate(parts, axis=0).astype(BF))
        g_x = g_x.T
        g_out[i] = scale * (inject * g_x)
        stores.append(start(g_out.at[i], g_far.at[i], sems.at[2 * images + len(pairs) + i]))
        u = u + jnp.sum(g_x * feature[i], axis=0, keepdims=True)
    u_out[...] = jnp.broadcast_to(u, u_out.shape)
    cross = jnp.sum(inject * u)
    payload[...] = jnp.broadcast_to(lane_row([(0, loss / denom), (1, cross)])[None], payload.shape)
    for copy in stores:
        copy.wait()


def back_kernel(
    g_far, feature_far, relu_far, w_two_far, x3_far, by_g, by_feature, x3,
    g, feature, relu, w_two, sems,
):
    images, tokens, channels = by_g.shape
    loads = [start(w_two_far, w_two, sems.at[0])]
    pairs = ((feature_far, feature), (relu_far, relu), (g_far, g), (x3_far, x3))
    for j, (far, near) in enumerate(pairs):
        loads.append(start(far, near, sems.at[1 + j]))
    for copy in loads[:3]:
        copy.wait()
    for i in range(images):
        back = mm_nt(feature[i].astype(BF), w_two[...])
        by_feature[i] = jnp.where(relu[i].astype(F32) > 0, back, 0.0)
    loads[3].wait()
    for i in range(images):
        back = mm_nt(g[i].astype(BF), w_two[...])
        by_g[i] = jnp.where(relu[i].astype(F32) > 0, back, 0.0)
    loads[4].wait()


def solve_kernel(
    cols, elements, place, sums, sums_two, by_g, by_feature, scalars, gz, to_pair, to_other
):
    images, tokens, channels = gz.shape
    scale = norm_of(jnp.sum(sums[...], axis=0), elements)
    line = jnp.sum(sums_two[...], axis=0)
    pull = scale * scale * scale * (lane_pick(line, 1) / elements)
    pairs = [(0, jnp.full((1, 1), lane_pick(line, 0), F32)), (1, pull), (2, scale)]
    scalars[...] = jnp.broadcast_to(lane_row(pairs), scalars.shape)
    for i in range(images):
        back = by_g[i] - pull * by_feature[i]
        gz[i] = back.astype(BF)
        top, bottom = back[:cols], back[tokens - cols :]
        pair, other = neighbours(place, top, bottom)
        to_pair[i], to_other[i] = pair.astype(BF), other.astype(BF)


def block_weight_kernel(
    cols, scalars, u, gz, x3, relu_far, g_far, feature_far,
    d_block, d_rows, g_f, relu, g, feature, sems,
):
    images, tokens, channels = gz.shape
    kept = 3 * channels
    late = [
        start(far, near, sems.at[j])
        for j, (far, near) in enumerate(((relu_far, relu), (g_far, g), (feature_far, feature)))
    ]
    pull, scale = scalars[0:1, 1:2], scalars[0:1, 2:3]
    rows = [jnp.zeros((1, channels), F32), jnp.zeros((1, channels), F32)]
    for i in range(images):
        for dy in range(3):
            at = slice(dy * kept, (dy + 1) * kept)
            part = mm_tn(x3[i, dy * cols : dy * cols + tokens], gz[i])
            d_block[at] = part if i == 0 else d_block[at] + part
        rows[0] = rows[0] + jnp.sum(gz[i].astype(F32), axis=0, keepdims=True)
    for copy in late:
        copy.wait()
    at = slice(3 * kept, 3 * kept + channels)
    for i in range(images):
        g_f[i] = g[i] - pull * feature[i]
        low = g_f[i].astype(BF)
        part = mm_tn(relu[i], low)
        d_block[at] = part if i == 0 else d_block[at] + part
        rows[1] = rows[1] + jnp.sum(low.astype(F32), axis=0, keepdims=True)
    d_rows[...] = jnp.concatenate(rows + [scale * u[0:1], jnp.zeros((5, channels), F32)], axis=0)


def pack_rows_of(plan, me, i, table, begin, keep, send):
    rows, split = plan.rows, plan.part_a
    k, at_a, at_b = plan.place(i, me)
    half = begin + rows // 2
    one = table[begin : begin + rows, :LANES]
    two = table[begin : begin + rows, LANES : 2 * LANES]
    tail = jnp.concatenate(
        [table[begin:half, 2 * LANES :], table[half : begin + rows, 2 * LANES :]], axis=1
    )
    a = jnp.concatenate([one, two[: split - rows]], axis=0).astype(BF)
    b = jnp.concatenate([two[split - rows :], tail], axis=0).astype(BF)
    for wanted, out in ((0, keep), (1, send)):
        hit = k == wanted
        out[jnp.where(hit, at_a, plan.half), :split] = a
        out[jnp.where(hit, at_b, plan.half), split:] = b


def input_kernel(
    plan, cols, place, gz, first, second, g_f, d_block, d_rows, w1t_far, c3_far,
    keep, send, table, w1t, c3, sems,
):
    me = place[0]
    images, tokens, channels = gz.shape
    kept, kept_in = 3 * channels, c3.shape[2]
    load = start(w1t_far, w1t, sems.at[0])
    late = start(c3_far, c3, sems.at[1])
    n_in, n_block = 3 * kept_in, d_block.shape[0]
    inner = [
        i for i in range(plan.count)
        if n_in <= plan.start[i] and plan.start[i] + plan.rows <= n_in + n_block
    ]
    outer = [i for i in range(plan.count) if i not in inner]
    for i in inner:
        pack_rows_of(plan, me, i, d_block, plan.start[i] - n_in, keep, send)
    for i in outer:
        low = max(plan.start[i], n_in) // 8 * 8
        high = min(-(-(plan.start[i] + plan.rows) // 8) * 8, n_in + n_block)
        if low < high:
            table[low:high] = d_block[low - n_in : high - n_in]
    wide = []
    for i in range(images):
        above, below = neighbours(place, first[i].astype(F32), second[i].astype(F32))
        part = jnp.concatenate([above, gz[i].astype(F32), below], axis=0)
        wide.append(three_columns(part, cols))
    load.wait()
    db_in = jnp.zeros((1, channels), F32)
    for i in range(images):
        total = g_f[i] + sum(
            mm(wide[i][dy * cols : dy * cols + tokens], w1t[dy * kept : (dy + 1) * kept])
            for dy in range(3)
        )
        low = total.astype(BF)
        db_in = db_in + jnp.sum(low.astype(F32), axis=0, keepdims=True)
        if i == 0:
            late.wait()
        for dy in range(3):
            at = slice(dy * kept_in, (dy + 1) * kept_in)
            part = mm_tn(c3[i, (1 + dy) * cols : (1 + dy) * cols + tokens], low)
            table[at] = part if i == 0 else table[at] + part
    at = n_in + n_block
    table[at : at + 8] = jnp.concatenate(
        [db_in, d_rows[0:3], jnp.zeros((4, channels), F32)], axis=0
    )
    for i in outer:
        pack_rows_of(plan, me, i, table, plan.start[i], keep, send)


def snr_weights(timesteps):
    beta_sched = np.linspace(0.00085**0.5, 0.012**0.5, 1000, dtype=np.float64) ** 2
    alpha_bar = np.cumprod(1.0 - beta_sched)
    snr_value = alpha_bar / (1.0 - alpha_bar)
    lookup = jnp.asarray(np.minimum(snr_value, SNR_CAP) / snr_value, F32)
    hit_table = timesteps[:, None] == jnp.arange(1000, dtype=jnp.int32)[None, :]
    return jnp.sum(jnp.where(hit_table, lookup[None, :], 0.0), axis=1)


def trade_rows(first, second):
    count = lax.axis_size("sp")
    near = [(i, i ^ 1) for i in range(count)]
    far = [(i, i + 1 if i % 2 else i - 1) for i in range(count)]
    far = [(i, j) for i, j in far if 0 <= j < count]
    return lax.ppermute(first, "sp", near), lax.ppermute(second, "sp", far)


def everywhere(payload):
    return lax.all_to_all(payload, ("sp", "hd"), 0, 0, tiled=True)


def body(
    cond, resid, context, noise, timesteps, step, query_weight, key_weight, value_weight,
    out_weight, pred_weight, master, first_moment, second_moment,
):
    images, row_count, cols, in_chan = cond.shape
    channels = resid.shape[-1]
    out_chan = noise.shape[-1]
    words = context.shape[2]
    tokens = row_count * cols
    all_tokens = images * tokens
    sp, hd = lax.axis_size("sp"), lax.axis_size("hd")
    plan = Plan(sp, hd, master.shape[0], channels)
    height = row_count * sp
    elements = images * hd * height * cols * channels
    heads = channels // HDIM
    n_in, n_one, n_two = 9 * in_chan, 9 * channels, channels
    at_sp = lax.axis_index("sp")
    place = jnp.stack(
        [
            at_sp * hd + lax.axis_index("hd"),
            (at_sp == 0).astype(jnp.int32),
            (at_sp == sp - 1).astype(jnp.int32),
            at_sp % 2,
        ]
    )
    snr = snr_weights(timesteps.reshape(-1))
    wide, kept, kept_in = tokens + 2 * cols, 3 * channels, 3 * in_chan

    def edges():
        top, bottom = cond[:, :2], cond[:, row_count - 2 :]
        even = at_sp % 2 == 0
        pair = trade_rows(jnp.where(even, bottom, top), jnp.where(even, top, bottom))
        return [rows.reshape(images, 2 * cols, in_chan) for rows in pair]

    def prepare(first, second):
        return call(
            functools.partial(prepare_kernel, cols, heads),
            [
                ((images, wide + 2 * cols, kept_in), BF),
                ((images, heads, room, HDIM), BF),
                ((images, heads, HDIM, room), BF),
                ((images, heads, room, HDIM), BF),
                ((images, heads, HDIM, room), BF),
                ((images, channels, tokens), BF),
                ((channels, channels), BF),
                ((channels, channels), BF),
            ],
            [
                place, cond.reshape(images, tokens, in_chan), first, second,
                context.reshape(images, words, -1), key_weight.T, value_weight.T,
                resid.reshape(images, tokens, channels), query_weight, out_weight,
            ],
            smem=(0,),
            free=(1, 4, 5, 6, 7, 8, 9),
            far_like=(0, 1, 2, 3, 4, 5, 6, 7),
            flops=4 << 30,
        )

    room = -(-words // 16) * 16
    gathered, prepared = gather_parameters(plan, master, edges, prepare)
    c3, keys, keys_t, values, values_t, resid_t, wq_t, wo_t = prepared
    line = ((plan.count, 1, LANES), F32)
    per_image = (images, tokens, channels)
    w1t, w_two, trailing, feature, relu_low, x3, payload = call(
        functools.partial(forward_kernel, plan, cols),
        [
            ((n_one, channels), BF),
            ((n_two, channels), BF),
            ((8, channels), F32),
            (per_image, F32),
            (per_image, BF),
            ((images, wide, kept), BF),
            line,
        ],
        [place, snr, *gathered, c3],
        scratch=[
            VMEM((plan.table, channels), F32),
            VMEM((n_in + n_one + n_two, channels), BF),
            VMEM((n_one, channels), BF),
            VMEM((images, wide + 2 * cols, kept_in), BF),
            VMEM(per_image, F32),
            VMEM(per_image, BF),
            VMEM((images, wide, kept), BF),
            DMA((2 + 4 * images,)),
        ],
        smem=(0, 1),
        far=(6,),
        far_out=(0, 1, 3, 4, 5),
        flops=4 << 30,
    )
    sums = everywhere(payload)
    square = (channels, channels)
    g, u, payload = call(
        functools.partial(
            attention_kernel, plan, (elements, height * cols * out_chan, words)
        ),
        [(per_image, F32), ((8, channels), F32), line],
        [
            snr, sums, trailing, jnp.transpose(noise, (0, 1, 3, 2)), pred_weight.T,
            feature, resid_t, wq_t, keys, values_t, wo_t, out_weight, values, keys_t, query_weight,
        ],
        scratch=[
            VMEM(per_image, F32),
            VMEM((images, channels, tokens), BF),
            VMEM(square, BF),
            VMEM((images, heads, room, HDIM), BF),
            VMEM((images, heads, HDIM, room), BF),
            VMEM(square, BF),
            VMEM(square, BF),
            VMEM((images, heads, room, HDIM), BF),
            VMEM((images, heads, HDIM, room), BF),
            VMEM(square, BF),
            VMEM(per_image, F32),
            DMA((3 * images + 8,)),
        ],
        smem=(0,),
        far=tuple(range(5, 15)),
        far_out=(0,),
        flops=4 << 30,
    )
    sums_two = everywhere(payload)
    by_g, by_feature, x3 = call(
        back_kernel,
        [(per_image, F32), (per_image, F32), ((images, wide, kept), BF)],
        [g, feature, relu_low, w_two, x3],
        scratch=[
            VMEM(per_image, F32),
            VMEM(per_image, F32),
            VMEM(per_image, BF),
            VMEM((channels, channels), BF),
            DMA((5,)),
        ],
        far=(0, 1, 2, 3, 4),
        flops=4 << 30,
    )
    scalars, gz, to_pair, to_other = call(
        functools.partial(solve_kernel, cols, elements),
        [
            ((8, LANES), F32),
            (per_image, BF),
            ((images, cols, channels), BF),
            ((images, cols, channels), BF),
        ],
        [place, sums, sums_two, by_g, by_feature],
        smem=(0,),
        flops=1 << 29,
    )
    first, second = trade_rows(to_pair, to_other)
    d_block, d_rows, g_f = call(
        functools.partial(block_weight_kernel, cols),
        [((n_one + n_two, channels), F32), ((8, channels), F32), (per_image, F32)],
        [scalars, u, gz, x3, relu_low, g, feature],
        scratch=[
            VMEM(per_image, BF),
            VMEM(per_image, F32),
            VMEM(per_image, F32),
            DMA((3,)),
        ],
        far=(4, 5, 6),
        flops=2 << 30,
    )
    keep, send = call(
        functools.partial(input_kernel, plan, cols),
        [
            ((plan.half + 1, plan.packed, LANES), BF),
            ((plan.half + 1, plan.packed, LANES), BF),
        ],
        [place, gz, first, second, g_f, d_block, d_rows, w1t, c3],
        scratch=[
            VMEM((plan.table, channels), F32),
            VMEM((n_one, channels), BF),
            VMEM((images, wide + 2 * cols, kept_in), BF),
            DMA((2,)),
        ],
        smem=(0,),
        far=(7, 8),
        flops=4 << 30,
    )
    grad_share = scatter_gradient(plan, keep, send)
    steps_done = step[0].astype(F32)
    first_new = BETA_ONE * first_moment + (1.0 - BETA_ONE) * grad_share
    second_new = BETA_TWO * second_moment + (1.0 - BETA_TWO) * grad_share * grad_share
    first_hat = first_new / (1.0 - BETA_ONE**steps_done)
    second_hat = second_new / (1.0 - BETA_TWO**steps_done)
    new_master = master - RATE * (first_hat / (jnp.sqrt(second_hat) + EPS_ADAM) + DECAY * master)
    return (scalars[0, 0], new_master, first_new, second_new)


def solution(mesh):
    shard = P(("sp", "hd"))
    placed = (
        P("hd", "sp", None, None),
        P("hd", "sp", None, None),
        P("hd", None, None, None),
        P("hd", "sp", None, None),
        P("hd", None),
        P(),
        P(),
        P(),
        P(),
        P(),
        P(),
        shard,
        shard,
        shard,
    )
    return jax.shard_map(
        body,
        mesh=mesh,
        in_specs=placed,
        out_specs=(P(), shard, shard, shard),
        check_vma=False,
    )
```

```python
import functools

import jax
import jax.numpy as jnp
import numpy as np
from jax import lax
from jax.experimental import pallas as pl
from jax.experimental.pallas import tpu as pltpu
from jax.sharding import PartitionSpec as P

HDIM = 40
LANES = 128
EPS_NORM = 1e-05
RATE = 0.05
DECAY = 0.01
BETA_ONE = 0.5
BETA_TWO = 0.5
EPS_ADAM = 1e-08
SNR_CAP = 5.0
VMEM, HBM, DMA = pltpu.VMEM, pltpu.HBM, pltpu.SemaphoreType.DMA
BF = jnp.bfloat16
F32 = jnp.float32


def mm(a, b):
    return jnp.dot(a, b, preferred_element_type=F32)


def mm_nt(a, b):
    return lax.dot_general(a, b, (((1,), (1,)), ((), ())), preferred_element_type=F32)


def mm_tn(a, b):
    return lax.dot_general(a, b, (((0,), (0,)), ((), ())), preferred_element_type=F32)


def call(
    kernel, outs, ins, scratch=(), far=(), far_out=(), smem=(), free=(), far_like=(), flops=0,
    limit=40,
):
    def space(i):
        return pltpu.SMEM if i in smem else pl.ANY if i in far else VMEM

    def hold(i, x):
        return x if i in smem or i in free else pltpu.with_memory_space_constraint(x, HBM if i in far else VMEM)

    return pl.pallas_call(
        kernel,
        out_shape=[
            jax.ShapeDtypeStruct(*o) if i in far_like else (HBM if i in far_out else VMEM)(*o)
            for i, o in enumerate(outs)
        ],
        in_specs=[pl.BlockSpec(memory_space=space(i)) for i in range(len(ins))],
        out_specs=[
            pl.BlockSpec(memory_space=pl.ANY if i in far_out else VMEM) for i in range(len(outs))
        ],
        scratch_shapes=list(scratch),
        compiler_params=pltpu.CompilerParams(vmem_limit_bytes=limit * 1024 * 1024),
        cost_estimate=pl.CostEstimate(flops=flops, bytes_accessed=1 << 20, transcendentals=0),
    )(*[hold(i, x) for i, x in enumerate(ins)])


def start(source, target, sem):
    copy = pltpu.make_async_copy(source, target, sem)
    copy.start()
    return copy


class Plan:
    def __init__(self, sp, hd, length, channels):
        self.sp, self.hd, self.count = sp, hd, sp * hd
        self.length, self.channels = length, channels
        self.start = [length * i // channels for i in range(self.count)]
        need = max(
            -(-(length * i % channels + length) // channels) for i in range(self.count)
        )
        self.rows = -(-need // 32) * 32
        self.packed = self.rows * channels // LANES
        self.part_a = -(-self.packed // 32) * 16
        self.part_b = self.packed - self.part_a
        self.table = -(-(self.start[-1] + self.rows) // 8) * 8
        self.nz, self.nx = max(sp // 2, 1), min(sp, 2)
        self.ny, self.nk = max(hd // 2, 1), min(hd, 2)
        self.group_z = ("sp", sp, self.nx, self.nz)
        self.group_x = ("sp", sp, 1, self.nx)
        self.group_y = ("hd", hd, self.nk, self.ny)
        self.group_k = ("hd", hd, 1, self.nk)
        self.half = self.count // self.nk

    def place(self, owner, me):
        off = owner ^ me
        off_sp, off_hd = off // self.hd, off % self.hd
        z, x = off_sp // self.nx, off_sp % self.nx
        y, k = off_hd // self.nk, off_hd % self.nk
        return k, (y * self.nx + x) * self.nz + z, (x * self.ny + y) * self.nz + z


def swap(value, group, step):
    axis, count, stride, _ = group
    return lax.ppermute(value, axis, [(i, i ^ (step * stride)) for i in range(count)])


def spread(block, group):
    return jnp.concatenate([block] + [swap(block, group, e) for e in range(1, group[3])], axis=0)


def collect(total, group):
    size = total.shape[0] // group[3]
    out = total[:size]
    for e in range(1, group[3]):
        out = out + swap(total[e * size : (e + 1) * size].astype(BF), group, e).astype(F32)
    return out


def pack_rows(table):
    rows = table.shape[0]
    tail = table[:, 2 * LANES :]
    tail = jnp.concatenate([tail[: rows // 2], tail[rows // 2 :]], axis=1)
    return jnp.concatenate([table[:, :LANES], table[:, LANES : 2 * LANES], tail], axis=0)


def unpack_rows(packed, rows):
    tail = packed[2 * rows :]
    half = tail.shape[1] // 2
    tail = jnp.concatenate([tail[:, :half], tail[:, half:]], axis=0)
    return jnp.concatenate([packed[:rows], packed[rows : 2 * rows], tail], axis=1)


def gather_parameters(plan, master, edges, prepare):
    me = lax.axis_index("sp") * plan.hd + lax.axis_index("hd")
    shift = lax.rem(me * plan.length, plan.channels)
    total = plan.rows * plan.channels
    flat = jnp.pad(master, (plan.channels, total - plan.length))
    flat = lax.dynamic_slice(flat, (plan.channels - shift,), (total,))
    packed = pack_rows(flat.reshape(plan.rows, plan.channels).astype(BF))[None]
    packed = spread(packed, plan.group_z)
    part_a, part_b = packed[:, : plan.part_a], packed[:, plan.part_a :]
    part_a, edges = lax.optimization_barrier((part_a, edges()))
    part_a, part_b = spread(part_a, plan.group_x), spread(part_b, plan.group_y)
    part_a, part_b = spread(part_a, plan.group_y), spread(part_b, plan.group_x)
    part_a, part_b, ready = lax.optimization_barrier((part_a, part_b, prepare(*edges)))
    if plan.nk == 1:
        return (part_a, part_a, part_b, part_b), ready
    other_a, other_b = swap(part_a, plan.group_k, 1), swap(part_b, plan.group_k, 1)
    return (part_a, other_a, part_b, other_b), ready


def scatter_gradient(plan, keep, send):
    total = keep[: plan.half].astype(F32)
    if plan.nk > 1:
        total = total + swap(send, plan.group_k, 1)[: plan.half].astype(F32)
    part_a, part_b = total[:, : plan.part_a], total[:, plan.part_a :]
    for group_a, group_b in (
        (plan.group_y, plan.group_x),
        (plan.group_x, plan.group_y),
    ):
        part_a, part_b = collect(part_a, group_a), collect(part_b, group_b)
    packed = collect(jnp.concatenate([part_a, part_b], axis=1), plan.group_z)[0]
    flat = unpack_rows(packed, plan.rows).reshape(-1)
    me = lax.axis_index("sp") * plan.hd + lax.axis_index("hd")
    shift = lax.rem(me * plan.length, plan.channels)
    return lax.dynamic_slice(flat, (shift,), (plan.length,))


def three_columns(values, cols):
    tokens = values.shape[0]
    col = lax.broadcasted_iota(jnp.int32, values.shape, 0) % cols
    left = jnp.where(col == 0, 0.0, pltpu.roll(values, 1, 0))
    right = jnp.where(col == cols - 1, 0.0, pltpu.roll(values, tokens - 1, 0))
    return jnp.concatenate([left, values, right], axis=1).astype(BF)


def neighbours(odd, first, second):
    even = jnp.full((1, 1), odd, jnp.int32) == 0
    return jnp.where(even, second, first), jnp.where(even, first, second)


def lane_pick(row, lane):
    ids = lax.broadcasted_iota(jnp.int32, row.shape, 1)
    return jnp.sum(jnp.where(ids == lane, row, 0.0))


def lane_row(pairs):
    ids = lax.broadcasted_iota(jnp.int32, (1, LANES), 1)
    row = jnp.zeros((1, LANES), F32)
    for lane, value in pairs:
        row = jnp.where(ids == lane, value, row)
    return row


def prepare_kernel(
    cols, heads, place, cond, first, second, context, wk_t, wv_t, resid, wq, wo,
    c3, keys, keys_t, values, values_t, resid_t, wq_t, wo_t,
):
    images = cond.shape[0]
    channels, words = wk_t.shape[0], context.shape[1]
    room = keys.shape[2]
    pad = jnp.zeros((channels, LANES - words), F32)
    for i in range(images):
        low, high = neighbours(place[3], first[i].astype(F32), second[i].astype(F32))
        wide = jnp.concatenate([low, cond[i].astype(F32), high], axis=0)
        c3[i] = three_columns(wide, cols)
        for weight, flat, tall in ((wk_t, keys, keys_t), (wv_t, values, values_t)):
            turned = jnp.concatenate([mm_nt(weight[...], context[i]), pad], axis=1)
            for h in range(heads):
                part = turned[h * HDIM : (h + 1) * HDIM]
                tall[i, h] = part[:, :room].astype(BF)
                part = jnp.concatenate([part, jnp.zeros((LANES - HDIM, LANES), F32)], axis=0)
                flat[i, h] = part.T[:room, :HDIM].astype(BF)
        resid_t[i] = resid[i].astype(F32).T.astype(BF)
    wq_t[...] = wq[...].astype(F32).T.astype(BF)
    wo_t[...] = wo[...].astype(F32).T.astype(BF)


def unpack_table(plan, me, own_a, other_a, own_b, other_b, table, owners):
    rows, split = plan.rows, plan.part_a
    for i in owners:
        k, at_a, at_b = plan.place(i, me)
        own = jnp.full((1, 1), k, jnp.int32) == 0
        a = jnp.where(own, own_a[at_a].astype(F32), other_a[at_a].astype(F32))
        b = jnp.where(own, own_b[at_b].astype(F32), other_b[at_b].astype(F32))
        begin = plan.start[i]
        old = table[begin : begin + 1, :] if i > 0 else None
        table[begin : begin + rows, :LANES] = a[:rows]
        table[begin : begin + rows, LANES : 2 * LANES] = jnp.concatenate(
            [a[rows:], b[: 2 * rows - split]], axis=0
        )
        tail = b[2 * rows - split :]
        table[begin : begin + rows // 2, 2 * LANES :] = tail[:, : LANES // 2]
        table[begin + rows // 2 : begin + rows, 2 * LANES :] = tail[:, LANES // 2 :]
        if i > 0:
            table[begin : begin + 1, :] += old


def forward_kernel(
    plan, cols, place, snr, own_a, other_a, own_b, other_b, c3_far,
    w1t_far, w_two_far, trailing, feature_far, relu_far, x3_far, payload,
    table, weights, w1t, c3, feature, relu_low, x3, sems,
):
    me, first, last = place[0], place[1], place[2]
    images, wide, kept_in = c3.shape
    load = [start(c3_far.at[i], c3.at[i], sems.at[i]) for i in range(images)]
    count, channels = weights.shape
    tokens = wide - 4 * cols
    more = tokens + 2 * cols
    kept = 3 * channels
    n_in = 3 * kept_in
    base_two = n_in + 3 * kept
    blocks = (own_a, other_a, own_b, other_b, table)
    early = [i for i in range(plan.count) if plan.start[i] < n_in]
    unpack_table(plan, me, *blocks, early)
    weights[:n_in] = table[:n_in].astype(BF)
    for copy in load:
        copy.wait()
    a_one = [
        mm(
            jnp.concatenate([c3[i, dy * cols : dy * cols + more] for dy in range(3)], axis=1),
            weights[:n_in],
        )
        for i in range(images)
    ]
    unpack_table(plan, me, *blocks, range(len(early), plan.count))
    weights[n_in:] = table[n_in:count].astype(BF)
    for row in range(9):
        at = n_in + (8 - row) * channels
        w1t[row * channels : (row + 1) * channels] = table[at : at + channels].T.astype(BF)
    first_store = start(w1t, w1t_far, sems.at[1 + 4 * images])
    stores = [first_store, start(weights.at[base_two : base_two + channels], w_two_far, sems.at[images])]
    trailing[...] = jnp.concatenate([table[count : count + 4], jnp.zeros((4, channels), F32)], axis=0)
    b_in, b_one, b_two = trailing[0:1], trailing[1:2], trailing[2:3]
    square = jnp.zeros((1, 1), F32)
    row = lax.broadcasted_iota(jnp.int32, (more, channels), 0) // cols
    outside = ((row == 0) & (first == 1)) | ((row == tokens // cols + 1) & (last == 1))
    for i in range(images):
        a_one[i] = a_one[i] + b_in
        a_low = jnp.where(outside, 0.0, a_one[i]).astype(BF).astype(F32)
        x3[i] = three_columns(a_low, cols)
        stores.append(start(x3.at[i], x3_far.at[i], sems.at[images + 1 + 3 * i]))
    for i in range(images):
        pre_relu = b_one + sum(
            mm(
                x3[i, dy * cols : dy * cols + tokens],
                weights[n_in + dy * kept : n_in + (dy + 1) * kept],
            )
            for dy in range(3)
        )
        relu = jnp.maximum(pre_relu, 0.0).astype(BF)
        relu_low[i] = relu
        stores.append(start(relu_low.at[i], relu_far.at[i], sems.at[images + 2 + 3 * i]))
        out = mm(relu, weights[base_two : base_two + channels]) + b_two
        out = out + a_one[i][cols : cols + tokens]
        feature[i] = out
        stores.append(start(feature.at[i], feature_far.at[i], sems.at[images + 3 + 3 * i]))
        square = square + jnp.sum(out * out)
    total = snr[0]
    for i in range(1, images):
        total = total + snr[i]
    line = lane_row([(0, square), (1, total)])
    payload[...] = jnp.broadcast_to(line[None], payload.shape)
    for copy in stores:
        copy.wait()


def norm_of(line, elements):
    return lax.rsqrt(jnp.full((1, 1), lane_pick(line, 0) / elements + EPS_NORM, F32))


def attention_kernel(
    plan, sizes, snr, sums, trailing, noise_t, wp_t,
    feature_far, resid_far, wqt_far, keys_far, valuest_far, wot_far, wo_far, values_far, keyst_far, wq_far,
    g_far, u_out, payload,
    feature, resid, wqt, keys, valuest, wot, wo, values, keyst, wq, g_out, sems,
):
    elements, loss_count, words = sizes
    images, tokens, channels = feature.shape
    heads, room = keys.shape[1:3]
    each = range(images)
    loads = [[], [], []]
    pairs = (
        (wqt_far, wqt, 0), (keys_far, keys, 0), (valuest_far, valuest, 1), (wot_far, wot, 1),
        (wo_far, wo, 2), (values_far, values, 2), (keyst_far, keyst, 2), (wq_far, wq, 2),
    )
    for i in each:
        loads[0].append(start(feature_far.at[i], feature.at[i], sems.at[2 * i]))
        loads[0].append(start(resid_far.at[i], resid.at[i], sems.at[2 * i + 1]))
    for j, (far, near, group) in enumerate(pairs):
        loads[group].append(start(far, near, sems.at[2 * images + j]))
    line = jnp.sum(sums[...], axis=0)
    scale = norm_of(line, elements)
    denom = lane_pick(line, 1) / plan.sp * loss_count
    inject = trailing[3:4]
    column = jnp.broadcast_to(inject, (LANES, channels)).T[:, 0:1] * scale
    root = HDIM ** (-0.5)
    out_chan, width = noise_t.shape[2:]
    spare = jnp.zeros((16 - out_chan, channels), F32)
    wide_pred = jnp.concatenate([wp_t[...].astype(F32), spare], axis=0).astype(BF)
    known = lax.broadcasted_iota(jnp.int32, (room, tokens), 0) < words
    for copy in loads[0]:
        copy.wait()
    injected, scores = [], []
    for i in each:
        injected.append(resid[i].astype(F32) + column * feature[i].T)
        query = mm(wqt[...], injected[i].astype(BF))
        parts = [query[h * HDIM : (h + 1) * HDIM].astype(BF) for h in range(heads)]
        scores.append([mm(keys[i, h], parts[h]) for h in range(heads)])
    attn = []
    for i in each:
        attn.append([])
        for h in range(heads):
            part = jnp.where(known, scores[i][h] * root, -1e30)
            part = jnp.exp(part - jnp.max(part, axis=0, keepdims=True))
            attn[i].append(part / jnp.sum(part, axis=0, keepdims=True))
    for copy in loads[1]:
        copy.wait()
    loss = jnp.zeros((1, 1), F32)
    g_y, g_attn = [], []
    for i in each:
        mixed = [mm(valuest[i, h], attn[i][h].astype(BF)) for h in range(heads)]
        after = injected[i] + mm(wot[...], jnp.concatenate(mixed, axis=0).astype(BF))
        pred = mm(wide_pred, after.astype(BF))
        noise = jnp.concatenate([noise_t[i, r] for r in range(tokens // width)], axis=1)
        noise = jnp.concatenate([noise, jnp.zeros((16 - out_chan, tokens), F32)], axis=0)
        error = pred - noise
        loss = loss + snr[i] * jnp.sum(error * error)
        g_pred = (2.0 * snr[i] / denom) * error
        g_y.append(mm_tn(wide_pred, g_pred.astype(BF)))
        if i == 0:
            for copy in loads[2]:
                copy.wait()
        g_mixed = mm(wo[...], g_y[i].astype(BF))
        parts = [g_mixed[h * HDIM : (h + 1) * HDIM].astype(BF) for h in range(heads)]
        g_attn.append([mm(values[i, h], parts[h]) for h in range(heads)])
    g_scores = []
    for i in each:
        g_scores.append([])
        for h in range(heads):
            inner = jnp.sum(attn[i][h] * g_attn[i][h], axis=0, keepdims=True)
            g_scores[i].append((attn[i][h] * (g_attn[i][h] - inner)).astype(BF))
    u = jnp.zeros((1, channels), F32)
    stores = []
    for i in each:
        parts = [mm(keyst[i, h], g_scores[i][h]) * root for h in range(heads)]
        g_x = g_y[i] + mm(wq[...], jnp.concatenate(parts, axis=0).astype(BF))
        g_x = g_x.T
        g_out[i] = scale * (inject * g_x)
        stores.append(start(g_out.at[i], g_far.at[i], sems.at[2 * images + len(pairs) + i]))
        u = u + jnp.sum(g_x * feature[i], axis=0, keepdims=True)
    u_out[...] = jnp.broadcast_to(u, u_out.shape)
    cross = jnp.sum(inject * u)
    payload[...] = jnp.broadcast_to(lane_row([(0, loss / denom), (1, cross)])[None], payload.shape)
    for copy in stores:
        copy.wait()


def back_kernel(
    g_far, feature_far, relu_far, w_two_far, x3_far, by_g, by_feature, x3,
    g, feature, relu, w_two, sems,
):
    images, tokens, channels = by_g.shape
    loads = [start(w_two_far, w_two, sems.at[0])]
    pairs = ((feature_far, feature), (relu_far, relu), (g_far, g), (x3_far, x3))
    for j, (far, near) in enumerate(pairs):
        loads.append(start(far, near, sems.at[1 + j]))
    for copy in loads[:3]:
        copy.wait()
    for i in range(images):
        back = mm_nt(feature[i].astype(BF), w_two[...])
        by_feature[i] = jnp.where(relu[i].astype(F32) > 0, back, 0.0)
    loads[3].wait()
    for i in range(images):
        back = mm_nt(g[i].astype(BF), w_two[...])
        by_g[i] = jnp.where(relu[i].astype(F32) > 0, back, 0.0)
    loads[4].wait()


def solve_kernel(
    cols, elements, sums, sums_two, by_g, by_feature, scalars, gz, to_pair, to_other
):
    images, tokens, channels = gz.shape
    scale = norm_of(jnp.sum(sums[...], axis=0), elements)
    line = jnp.sum(sums_two[...], axis=0)
    pull = scale * scale * scale * (lane_pick(line, 1) / elements)
    pairs = [(0, jnp.full((1, 1), lane_pick(line, 0), F32)), (1, pull), (2, scale)]
    scalars[...] = jnp.broadcast_to(lane_row(pairs), scalars.shape)
    odd = lax.rem(lax.axis_index("sp"), 2)
    top = pl.multiple_of(odd * (tokens - cols), cols)
    bottom = pl.multiple_of((1 - odd) * (tokens - cols), cols)
    for i in range(images):
        gz[i] = (by_g[i] - pull * by_feature[i]).astype(BF)
        to_pair[i] = gz[i, pl.ds(bottom, cols)]
        to_other[i] = gz[i, pl.ds(top, cols)]


def block_weight_kernel(
    cols, scalars, u, gz, x3, relu_far, g_far, feature_far,
    d_block, d_rows, g_f, relu, g, feature, sems,
):
    images, tokens, channels = gz.shape
    kept = 3 * channels
    late = [
        start(far, near, sems.at[j])
        for j, (far, near) in enumerate(((relu_far, relu), (g_far, g), (feature_far, feature)))
    ]
    pull, scale = scalars[0:1, 1:2], scalars[0:1, 2:3]
    rows = [jnp.zeros((1, channels), F32), jnp.zeros((1, channels), F32)]
    for i in range(images):
        for dy in range(3):
            at = slice(dy * kept, (dy + 1) * kept)
            part = mm_tn(x3[i, dy * cols : dy * cols + tokens], gz[i])
            d_block[at] = part if i == 0 else d_block[at] + part
        rows[0] = rows[0] + jnp.sum(gz[i].astype(F32), axis=0, keepdims=True)
    for copy in late:
        copy.wait()
    at = slice(3 * kept, 3 * kept + channels)
    for i in range(images):
        g_f[i] = g[i] - pull * feature[i]
        low = g_f[i].astype(BF)
        part = mm_tn(relu[i], low)
        d_block[at] = part if i == 0 else d_block[at] + part
        rows[1] = rows[1] + jnp.sum(low.astype(F32), axis=0, keepdims=True)
    d_rows[...] = jnp.concatenate(rows + [scale * u[0:1], jnp.zeros((5, channels), F32)], axis=0)


def pack_rows_of(plan, me, i, table, begin, keep, send):
    rows, split = plan.rows, plan.part_a
    k, at_a, at_b = plan.place(i, me)
    half = begin + rows // 2
    one = table[begin : begin + rows, :LANES]
    two = table[begin : begin + rows, LANES : 2 * LANES]
    tail = jnp.concatenate(
        [table[begin:half, 2 * LANES :], table[half : begin + rows, 2 * LANES :]], axis=1
    )
    a = jnp.concatenate([one, two[: split - rows]], axis=0).astype(BF)
    b = jnp.concatenate([two[split - rows :], tail], axis=0).astype(BF)
    for wanted, out in ((0, keep), (1, send)):
        hit = k == wanted
        out[jnp.where(hit, at_a, plan.half), :split] = a
        out[jnp.where(hit, at_b, plan.half), split:] = b


def input_kernel(
    plan, cols, gz, first, second, g_f, d_block, d_rows, w1t_far, c3_far,
    keep, send, table, w1t, c3, sems,
):
    me = lax.axis_index("sp") * plan.hd + lax.axis_index("hd")
    images, tokens, channels = gz.shape
    kept, kept_in = 3 * channels, c3.shape[2]
    load = start(w1t_far, w1t, sems.at[0])
    late = start(c3_far, c3, sems.at[1])
    n_in, n_block = 3 * kept_in, d_block.shape[0]
    inner = [
        i for i in range(plan.count)
        if n_in <= plan.start[i] and plan.start[i] + plan.rows <= n_in + n_block
    ]
    outer = [i for i in range(plan.count) if i not in inner]
    for i in inner:
        pack_rows_of(plan, me, i, d_block, plan.start[i] - n_in, keep, send)
    for i in outer:
        low = max(plan.start[i], n_in) // 8 * 8
        high = min(-(-(plan.start[i] + plan.rows) // 8) * 8, n_in + n_block)
        if low < high:
            table[low:high] = d_block[low - n_in : high - n_in]
    wide = []
    for i in range(images):
        above, below = neighbours(lax.rem(lax.axis_index("sp"), 2), first[i].astype(F32), second[i].astype(F32))
        part = jnp.concatenate([above, gz[i].astype(F32), below], axis=0)
        wide.append(three_columns(part, cols))
    load.wait()
    db_in = jnp.zeros((1, channels), F32)
    for i in range(images):
        total = g_f[i] + sum(
            mm(wide[i][dy * cols : dy * cols + tokens], w1t[dy * kept : (dy + 1) * kept])
            for dy in range(3)
        )
        low = total.astype(BF)
        db_in = db_in + jnp.sum(low.astype(F32), axis=0, keepdims=True)
        if i == 0:
            late.wait()
        for dy in range(3):
            at = slice(dy * kept_in, (dy + 1) * kept_in)
            part = mm_tn(c3[i, (1 + dy) * cols : (1 + dy) * cols + tokens], low)
            table[at] = part if i == 0 else table[at] + part
    at = n_in + n_block
    table[at : at + 8] = jnp.concatenate(
        [db_in, d_rows[0:3], jnp.zeros((4, channels), F32)], axis=0
    )
    for i in outer:
        pack_rows_of(plan, me, i, table, plan.start[i], keep, send)


def snr_weights(timesteps):
    beta_sched = np.linspace(0.00085**0.5, 0.012**0.5, 1000, dtype=np.float64) ** 2
    alpha_bar = np.cumprod(1.0 - beta_sched)
    snr_value = alpha_bar / (1.0 - alpha_bar)
    lookup = jnp.asarray(np.minimum(snr_value, SNR_CAP) / snr_value, F32)
    hit_table = timesteps[:, None] == jnp.arange(1000, dtype=jnp.int32)[None, :]
    return jnp.sum(jnp.where(hit_table, lookup[None, :], 0.0), axis=1)


def trade_rows(first, second):
    count = lax.axis_size("sp")
    near = [(i, i ^ 1) for i in range(count)]
    far = [(i, i + 1 if i % 2 else i - 1) for i in range(count)]
    far = [(i, j) for i, j in far if 0 <= j < count]
    return lax.ppermute(first, "sp", near), lax.ppermute(second, "sp", far)


def everywhere(payload):
    return lax.all_to_all(payload, ("sp", "hd"), 0, 0, tiled=True)


def body(
    cond, resid, context, noise, timesteps, step, query_weight, key_weight, value_weight,
    out_weight, pred_weight, master, first_moment, second_moment,
):
    images, row_count, cols, in_chan = cond.shape
    channels = resid.shape[-1]
    out_chan = noise.shape[-1]
    words = context.shape[2]
    tokens = row_count * cols
    all_tokens = images * tokens
    sp, hd = lax.axis_size("sp"), lax.axis_size("hd")
    plan = Plan(sp, hd, master.shape[0], channels)
    height = row_count * sp
    elements = images * hd * height * cols * channels
    heads = channels // HDIM
    n_in, n_one, n_two = 9 * in_chan, 9 * channels, channels
    at_sp = lax.axis_index("sp")
    place = jnp.stack(
        [
            at_sp * hd + lax.axis_index("hd"),
            (at_sp == 0).astype(jnp.int32),
            (at_sp == sp - 1).astype(jnp.int32),
            at_sp % 2,
        ]
    )
    snr = snr_weights(timesteps.reshape(-1))
    wide, kept, kept_in = tokens + 2 * cols, 3 * channels, 3 * in_chan

    def edges():
        top, bottom = cond[:, :2], cond[:, row_count - 2 :]
        even = at_sp % 2 == 0
        pair = trade_rows(jnp.where(even, bottom, top), jnp.where(even, top, bottom))
        return [rows.reshape(images, 2 * cols, in_chan) for rows in pair]

    def prepare(first, second):
        return call(
            functools.partial(prepare_kernel, cols, heads),
            [
                ((images, wide + 2 * cols, kept_in), BF),
                ((images, heads, room, HDIM), BF),
                ((images, heads, HDIM, room), BF),
                ((images, heads, room, HDIM), BF),
                ((images, heads, HDIM, room), BF),
                ((images, channels, tokens), BF),
                ((channels, channels), BF),
                ((channels, channels), BF),
            ],
            [
                place, cond.reshape(images, tokens, in_chan), first, second,
                context.reshape(images, words, -1), key_weight.T, value_weight.T,
                resid.reshape(images, tokens, channels), query_weight, out_weight,
            ],
            smem=(0,),
            free=(1, 4, 5, 6, 7, 8, 9),
            far_like=(0, 1, 2, 3, 4, 5, 6, 7),
            flops=4 << 30,
        )

    room = -(-words // 16) * 16
    gathered, prepared = gather_parameters(plan, master, edges, prepare)
    c3, keys, keys_t, values, values_t, resid_t, wq_t, wo_t = prepared
    line = ((plan.count, 1, LANES), F32)
    per_image = (images, tokens, channels)
    w1t, w_two, trailing, feature, relu_low, x3, payload = call(
        functools.partial(forward_kernel, plan, cols),
        [
            ((n_one, channels), BF),
            ((n_two, channels), BF),
            ((8, channels), F32),
            (per_image, F32),
            (per_image, BF),
            ((images, wide, kept), BF),
            line,
        ],
        [place, snr, *gathered, c3],
        scratch=[
            VMEM((plan.table, channels), F32),
            VMEM((n_in + n_one + n_two, channels), BF),
            VMEM((n_one, channels), BF),
            VMEM((images, wide + 2 * cols, kept_in), BF),
            VMEM(per_image, F32),
            VMEM(per_image, BF),
            VMEM((images, wide, kept), BF),
            DMA((2 + 4 * images,)),
        ],
        smem=(0, 1),
        far=(6,),
        far_out=(0, 1, 3, 4, 5),
        flops=4 << 30,
    )
    sums = everywhere(payload)
    square = (channels, channels)
    g, u, payload = call(
        functools.partial(
            attention_kernel, plan, (elements, height * cols * out_chan, words)
        ),
        [(per_image, F32), ((8, channels), F32), line],
        [
            snr, sums, trailing, jnp.transpose(noise, (0, 1, 3, 2)), pred_weight.T,
            feature, resid_t, wq_t, keys, values_t, wo_t, out_weight, values, keys_t, query_weight,
        ],
        scratch=[
            VMEM(per_image, F32),
            VMEM((images, channels, tokens), BF),
            VMEM(square, BF),
            VMEM((images, heads, room, HDIM), BF),
            VMEM((images, heads, HDIM, room), BF),
            VMEM(square, BF),
            VMEM(square, BF),
            VMEM((images, heads, room, HDIM), BF),
            VMEM((images, heads, HDIM, room), BF),
            VMEM(square, BF),
            VMEM(per_image, F32),
            DMA((3 * images + 8,)),
        ],
        smem=(0,),
        far=tuple(range(5, 15)),
        far_out=(0,),
        flops=4 << 30,
    )
    sums_two = everywhere(payload)
    by_g, by_feature, x3 = call(
        back_kernel,
        [(per_image, F32), (per_image, F32), ((images, wide, kept), BF)],
        [g, feature, relu_low, w_two, x3],
        scratch=[
            VMEM(per_image, F32),
            VMEM(per_image, F32),
            VMEM(per_image, BF),
            VMEM((channels, channels), BF),
            DMA((5,)),
        ],
        far=(0, 1, 2, 3, 4),
        flops=4 << 30,
    )
    scalars, gz, to_pair, to_other = call(
        functools.partial(solve_kernel, cols, elements),
        [
            ((8, LANES), F32),
            (per_image, BF),
            ((images, cols, channels), BF),
            ((images, cols, channels), BF),
        ],
        [sums, sums_two, by_g, by_feature],
        flops=1 << 29,
    )
    first, second = trade_rows(to_pair, to_other)
    d_block, d_rows, g_f = call(
        functools.partial(block_weight_kernel, cols),
        [((n_one + n_two, channels), F32), ((8, channels), F32), (per_image, F32)],
        [scalars, u, gz, x3, relu_low, g, feature],
        scratch=[
            VMEM(per_image, BF),
            VMEM(per_image, F32),
            VMEM(per_image, F32),
            DMA((3,)),
        ],
        far=(4, 5, 6),
        flops=2 << 30,
    )
    keep, send = call(
        functools.partial(input_kernel, plan, cols),
        [
            ((plan.half + 1, plan.packed, LANES), BF),
            ((plan.half + 1, plan.packed, LANES), BF),
        ],
        [gz, first, second, g_f, d_block, d_rows, w1t, c3],
        scratch=[
            VMEM((plan.table, channels), F32),
            VMEM((n_one, channels), BF),
            VMEM((images, wide + 2 * cols, kept_in), BF),
            DMA((2,)),
        ],
        far=(6, 7),
        flops=4 << 30,
    )
    grad_share = scatter_gradient(plan, keep, send)
    steps_done = step[0].astype(F32)
    first_new = BETA_ONE * first_moment + (1.0 - BETA_ONE) * grad_share
    second_new = BETA_TWO * second_moment + (1.0 - BETA_TWO) * grad_share * grad_share
    first_hat = first_new / (1.0 - BETA_ONE**steps_done)
    second_hat = second_new / (1.0 - BETA_TWO**steps_done)
    new_master = master - RATE * (first_hat / (jnp.sqrt(second_hat) + EPS_ADAM) + DECAY * master)
    return (scalars[0, 0], new_master, first_new, second_new)


def solution(mesh):
    shard = P(("sp", "hd"))
    placed = (
        P("hd", "sp", None, None),
        P("hd", "sp", None, None),
        P("hd", None, None, None),
        P("hd", "sp", None, None),
        P("hd", None),
        P(),
        P(),
        P(),
        P(),
        P(),
        P(),
        shard,
        shard,
        shard,
    )
    return jax.shard_map(
        body,
        mesh=mesh,
        in_specs=placed,
        out_specs=(P(), shard, shard, shard),
        check_vma=False,
    )
```
